256 devices in a mesh: row: 16 (over y, z_lo), col: 16 (over x, z_hi, core).
Axes of the slice: x: 4, y: 4, z: 8 (z_hi: 2, z_lo: 4; z = z_hi * 4 + z_lo), core: 2. Of those that a mesh axis runs over, the one named last changes fastest.
Arguments:
- right_side: float32 [64, 32768], P(None, ('row', 'col')), may hold values from -40 to 40
- points: float32 [2, 32768], P(None, ('row', 'col')), may hold values from 0 to 1
- star_noise: float32 [32768], P(('row', 'col')), may hold values from 0.5 to 2
Outputs:
- solution_field: float32 [64, 32768], P(None, ('row', 'col'))
- residual: float32 [64, 32768], P(None, ('row', 'col'))
The draws below stay inside these ranges and needn't reach their ends.
All inputs are finite; a program needn't handle non-finite values.
Results may differ from the reference program's by a relative error of at most 0.0003.
Values sent between devices are 32-bit elements; how exact they have to be, the bound alone decides.
No kernel may reach another device: no remote copies, remote signals or barrier semaphores. Data moves between devices by JAX's collectives and lax.ppermute only.
A program may use at most 64 MiB of HBM per device.

```python
import math
import jax
import jax.numpy as jnp
from jax import lax

RHS = 64
ITERS = 3
STARS = 32768


def draw_right_side(key, part):
    key = jax.random.fold_in(key, 7)
    position = jnp.arange(STARS, dtype=jnp.float32) / STARS
    scale = 10.0 ** position
    values = jnp.clip(jax.random.normal(key, (RHS, STARS), jnp.float32), -4.0, 4.0)
    return values * scale[None, :]


def steps_of(stream_key, dims, split, least, largest):
    level = 1.0
    for dim, blocks in split:
        draws = jax.random.uniform(jax.random.fold_in(jax.random.fold_in(stream_key, 6), dim), (blocks,), jnp.float32, least / len(split), largest / len(split))
        level = level * jnp.repeat(jnp.exp(draws), dims[dim] // blocks).reshape((-1,) + (1,) * (len(dims) - 1 - dim))
    return level


def setup_inputs(seed: int = 0) -> dict:
    keys = jax.random.split(jax.random.key(seed), 4)
    return {
        "right_side": draw_right_side(jax.random.fold_in(keys[3], 71), 0),
        "points": jnp.clip(1.0 * jax.random.uniform(keys[1], (2, STARS), jnp.float32) ** steps_of(keys[1], (2, STARS), ((1, 256),), -0.2, 0.2), 0.0, 1.0),
        "star_noise": jnp.clip(jnp.exp(math.log(2.0) - 1.3862944 * jax.random.uniform(keys[2], (STARS,), jnp.float32) ** steps_of(keys[2], (STARS,), ((0, 256),), -0.2, 0.2)), 0.5, 2.0),
    }


QUAD_XX = 1.6
QUAD_XY = 0.5
QUAD_YY = 0.7
INVERSE_SQUARE = 25.0
KERNEL_WEIGHT = 2048.0

def kernel_block(row_points, column_points, amplitude):
    delta_x = row_points[0][:, None] - column_points[0][None, :]
    delta_y = row_points[1][:, None] - column_points[1][None, :]
    quadratic = (QUAD_XX * delta_x * delta_x + 2.0 * QUAD_XY * delta_x * delta_y + QUAD_YY * delta_y * delta_y) * INVERSE_SQUARE
    return amplitude * jnp.exp(-jnp.sqrt(quadratic))

def contract(vectors, kernel_tile):
    return lax.dot_general(vectors, kernel_tile, (((1,), (1,)), ((), ())), precision=lax.Precision.HIGHEST, preferred_element_type=jnp.float32)

def operate(vectors, points, star_noise):
    block_rows = math.gcd(STARS, 1024)
    block_count = STARS // block_rows
    amplitude = KERNEL_WEIGHT / STARS

    def row_block(index):
        offset = (index * block_rows).astype(jnp.int32)
        row_points = lax.dynamic_slice_in_dim(points, offset, block_rows, 1)
        return contract(vectors, kernel_block(row_points, points, amplitude))
    stacked = lax.map(row_block, jnp.arange(block_count, dtype=jnp.int32))
    products = jnp.transpose(stacked, (1, 0, 2)).reshape(vectors.shape[0], STARS)
    return products + star_noise[None, :] * vectors

def reference(right_side, points, star_noise):
    solution_field = jnp.zeros_like(right_side)
    residual = right_side
    direction = right_side
    norm_now = lax.optimization_barrier(jnp.sum(residual * residual, axis=1, keepdims=True))
    for iteration in range(ITERS):
        applied = operate(direction, points, star_noise)
        step_size = norm_now / lax.optimization_barrier(jnp.sum(direction * applied, axis=1, keepdims=True))
        solution_field = solution_field + step_size * direction
        residual = residual - step_size * applied
        norm_next = lax.optimization_barrier(jnp.sum(residual * residual, axis=1, keepdims=True))
        direction = residual + norm_next / norm_now * direction
        norm_now = norm_next
    return (solution_field, residual)
```

```python
import functools
import math

import jax
import jax.numpy as jnp
from jax import lax
from jax.experimental import pallas as pl
from jax.experimental.pallas import tpu as pltpu
from jax.sharding import PartitionSpec as P

QUAD_XX = 1.6
QUAD_XY = 0.5
QUAD_YY = 0.7
INVERSE_SQUARE = 25.0
KERNEL_WEIGHT = 2048.0

PX = math.sqrt(QUAD_XX * INVERSE_SQUARE)
PY = QUAD_XY * INVERSE_SQUARE / PX
QY = math.sqrt(QUAD_YY * INVERSE_SQUARE - PY * PY)

AXES = ("row", "col")
LANES = 128
SPARE = 8
TILE = 256
VMEM_LIMIT = 24 * 1024 * 1024

ROUNDS_A = (("z", (3, 2, 1)), ("y", (2, 1, 3)))
ROUNDS_B = (("z", (7,)), ("x", (2, 1, 3)), ("core", (1,)))


def place(index):
    row, col = divmod(index, 16)
    y, z_lo = divmod(row, 4)
    x, rest = divmod(col, 4)
    z_hi, core = divmod(rest, 2)
    return {"x": x, "y": y, "z": z_hi * 4 + z_lo, "core": core}


def number(at):
    row = at["y"] * 4 + at["z"] % 4
    return row * 16 + at["x"] * 4 + (at["z"] // 4) * 2 + at["core"]


def exchange(value, axis, mask):
    pairs = []
    for index in range(256):
        at = place(index)
        at[axis] ^= mask
        pairs.append((index, number(at)))
    return lax.ppermute(value, AXES, pairs)


def gather(block, rounds):
    for axis, masks in rounds:
        block = jnp.concatenate([block] + [exchange(block, axis, m) for m in masks], axis=0)
    return block


def scatter_sum(blocks, rounds):
    for axis, masks in reversed(rounds):
        rows = blocks.shape[0] // (len(masks) + 1)
        total = blocks[:rows]
        for i, m in enumerate(masks):
            total = total + exchange(blocks[(i + 1) * rows : (i + 2) * rows], axis, m)
        blocks = total
    return blocks


def all_sum(block):
    for axis, masks in ROUNDS_B + ROUNDS_A:
        block = block + sum(exchange(block, axis, m) for m in masks)
    return block


def split(vectors):
    high = vectors.astype(jnp.bfloat16)
    low = (vectors - high.astype(jnp.float32)).astype(jnp.bfloat16)
    return high, low


def unpack(v_ref, pair_ref, dots_ref, rhs):
    total = jnp.zeros((SPARE, LANES), jnp.float32)
    step = rhs + SPARE
    for b in range(v_ref.shape[0] // step):
        high, low = split(v_ref[b * step : b * step + rhs, :])
        pair_ref[:rhs, b * LANES : (b + 1) * LANES] = high
        pair_ref[rhs:, b * LANES : (b + 1) * LANES] = low
        total = total + v_ref[b * step + rhs : (b + 1) * step, :]
    dots_ref[...] = total


def emit(out_ref, product, dots, rhs, amplitude):
    step = rhs + SPARE
    for piece in range(product.shape[1] // LANES):
        out_ref[piece * step : piece * step + rhs, :] = (
            product[:, piece * LANES : (piece + 1) * LANES] * amplitude
        )
        out_ref[piece * step + rhs : (piece + 1) * step, :] = dots


def first_kernel(rhs, amplitude, v_ref, rows_ref, out_ref, high_ref, low_ref, pair_ref, dots_ref, points_ref):
    step = rhs + SPARE
    stars = high_ref.shape[1]

    @pl.when(pl.program_id(0) == 0)
    def _():
        unpack(v_ref, pair_ref, dots_ref, rhs)
        for b in range(stars // LANES):
            tile = v_ref[b * step + rhs : (b + 1) * step, :]
            square = jnp.concatenate([tile, jnp.zeros((LANES - SPARE, LANES), jnp.float32)], axis=0)
            points_ref[b * LANES : (b + 1) * LANES, :] = square.T

    row_x = jnp.concatenate([rows_ref[0:1, :], rows_ref[SPARE : SPARE + 1, :]], axis=1)
    row_y = jnp.concatenate([rows_ref[1:2, :], rows_ref[SPARE + 1 : SPARE + 2, :]], axis=1)
    row_p = PX * row_x + PY * row_y
    row_q = QY * row_y
    product = jnp.zeros((rhs, TILE), jnp.float32)
    for j in range(0, stars, TILE):
        x = points_ref[j : j + TILE, 0:1]
        y = points_ref[j : j + TILE, 1:2]
        delta_p = (PX * x + PY * y) - row_p
        delta_q = QY * y - row_q
        square = delta_p * delta_p + delta_q * delta_q
        distance = square * lax.rsqrt(jnp.maximum(square, 1e-30))
        high, low = split(jnp.exp(-distance))
        high_ref[0, j : j + TILE, :] = high
        low_ref[0, j : j + TILE, :] = low
        both = jnp.dot(pair_ref[:, j : j + TILE], high, preferred_element_type=jnp.float32)
        rest = jnp.dot(pair_ref[:rhs, j : j + TILE], low, preferred_element_type=jnp.float32)
        product = product + (both[:rhs] + (both[rhs:] + rest))
    emit(out_ref, product, dots_ref[...], rhs, amplitude)


def next_kernel(rhs, amplitude, v_ref, high_ref, low_ref, out_ref, pair_ref, dots_ref):
    @pl.when(pl.program_id(0) == 0)
    def _():
        unpack(v_ref, pair_ref, dots_ref, rhs)

    both = jnp.dot(pair_ref[...], high_ref[0], preferred_element_type=jnp.float32)
    rest = jnp.dot(pair_ref[:rhs, :], low_ref[0], preferred_element_type=jnp.float32)
    emit(out_ref, both[:rhs] + (both[rhs:] + rest), dots_ref[...], rhs, amplitude)


def first_product(gathered, row_points, rhs, amplitude):
    blocks = gathered.shape[0] // (rhs + SPARE)
    stars = blocks * LANES
    tiles = row_points.shape[0] // SPARE * LANES // TILE
    per = TILE // LANES
    return pl.pallas_call(
        functools.partial(first_kernel, rhs, amplitude),
        grid=(tiles,),
        in_specs=[
            pl.BlockSpec(gathered.shape, lambda i: (0, 0)),
            pl.BlockSpec((per * SPARE, LANES), lambda i: (i, 0)),
        ],
        out_specs=[
            pl.BlockSpec((per * (rhs + SPARE), LANES), lambda i: (i, 0)),
            pl.BlockSpec((1, stars, TILE), lambda i: (i, 0, 0)),
            pl.BlockSpec((1, stars, TILE), lambda i: (i, 0, 0)),
        ],
        out_shape=[
            jax.ShapeDtypeStruct((tiles * per * (rhs + SPARE), LANES), jnp.float32),
            jax.ShapeDtypeStruct((tiles, stars, TILE), jnp.bfloat16),
            jax.ShapeDtypeStruct((tiles, stars, TILE), jnp.bfloat16),
        ],
        scratch_shapes=[
            pltpu.VMEM((2 * rhs, stars), jnp.bfloat16),
            pltpu.VMEM((SPARE, LANES), jnp.float32),
            pltpu.VMEM((stars, LANES), jnp.float32),
        ],
        compiler_params=pltpu.CompilerParams(vmem_limit_bytes=VMEM_LIMIT),
    )(gathered, row_points)


def next_product(gathered, high, low, rhs, amplitude):
    tiles, stars, _ = high.shape
    per = TILE // LANES
    return pl.pallas_call(
        functools.partial(next_kernel, rhs, amplitude),
        grid=(tiles,),
        in_specs=[
            pl.BlockSpec(gathered.shape, lambda i: (0, 0)),
            pl.BlockSpec((1, stars, TILE), lambda i: (i, 0, 0)),
            pl.BlockSpec((1, stars, TILE), lambda i: (i, 0, 0)),
        ],
        out_specs=pl.BlockSpec((per * (rhs + SPARE), LANES), lambda i: (i, 0)),
        out_shape=jax.ShapeDtypeStruct((tiles * per * (rhs + SPARE), LANES), jnp.float32),
        scratch_shapes=[
            pltpu.VMEM((2 * rhs, stars), jnp.bfloat16),
            pltpu.VMEM((SPARE, LANES), jnp.float32),
        ],
        compiler_params=pltpu.CompilerParams(vmem_limit_bytes=VMEM_LIMIT),
    )(gathered, high, low)


def dot(a, b):
    return jnp.sum(a * b, axis=1, keepdims=True)


def to_rows(columns, rhs):
    lane = lax.broadcasted_iota(jnp.int32, (rhs, LANES), 1)
    tile = jnp.zeros((rhs, LANES), jnp.float32)
    for i, column in enumerate(columns):
        tile = jnp.where(lane == i, column, tile)
    square = jnp.concatenate([tile, jnp.zeros((LANES - rhs, LANES), jnp.float32)], axis=0)
    return square.T[:SPARE, :]


def to_columns(tile, count, rhs):
    square = jnp.concatenate([tile, jnp.zeros((LANES - SPARE, LANES), jnp.float32)], axis=0).T
    return [square[:rhs, i : i + 1] for i in range(count)]


def update_one(rhs, sums_ref, right_ref, noise_ref, out_ref):
    right = right_ref[...]
    image = sums_ref[:rhs, :] + noise_ref[...] * right
    out_ref[:rhs, :] = image
    out_ref[rhs:, :] = to_rows([dot(right, right), dot(right, image)], rhs)


def update_two(rhs, sums_ref, right_ref, first_ref, noise_ref, out_ref, second_ref, scalars_ref):
    right = right_ref[...]
    w0 = first_ref[:rhs, :]
    n0 = sums_ref[:rhs, :] + noise_ref[...] * w0
    norm, curve = to_columns(sums_ref[rhs:, :], 2, rhs)
    alpha = norm / curve
    r1 = right - alpha * w0
    w1 = w0 - alpha * n0
    out_ref[:rhs, :] = w1
    out_ref[rhs:, :] = to_rows([dot(r1, r1), dot(r1, w1)], rhs)
    second_ref[...] = n0
    scalars_ref[...] = sums_ref[rhs:, :]


def update_three(rhs, sums_ref, right_ref, first_ref, second_ref, third_ref, scalars_ref, noise_ref, dots_ref, carry_ref):
    right = right_ref[...]
    w0 = first_ref[:rhs, :]
    n0 = second_ref[...]
    w1 = third_ref[:rhs, :]
    n1 = sums_ref[:rhs, :] + noise_ref[...] * w1
    norm0, curve0 = to_columns(scalars_ref[...], 2, rhs)
    norm1, curve1 = to_columns(sums_ref[rhs:, :], 2, rhs)
    alpha0 = norm0 / curve0
    beta1 = norm1 / norm0
    alpha1 = norm1 / (curve1 - beta1 * norm1 / alpha0)
    r1 = right - alpha0 * w0
    s1 = w1 + beta1 * w0
    p1 = r1 + beta1 * right
    z1 = n1 + beta1 * n0
    r2 = r1 - alpha1 * s1
    w2 = w1 - alpha1 * z1
    dots_ref[...] = to_rows([dot(r2, r2), dot(r2, w2)], rhs)
    lane = lax.broadcasted_iota(jnp.int32, (rhs, LANES), 1)
    carry_ref[0] = alpha0 * right + alpha1 * p1
    carry_ref[1] = r2
    carry_ref[2] = p1
    carry_ref[3] = s1
    carry_ref[4] = w2
    carry_ref[5] = jnp.where(lane == 0, alpha1, norm1)


def update_four(rhs, dots_ref, carry_ref, solution_ref, residual_ref):
    norm2, curve2 = to_columns(dots_ref[...], 2, rhs)
    alpha1 = carry_ref[5, :, 0:1]
    norm1 = carry_ref[5, :, 1:2]
    r2 = carry_ref[1]
    beta2 = norm2 / norm1
    alpha2 = norm2 / (curve2 - beta2 * norm2 / alpha1)
    solution_ref[...] = carry_ref[0] + alpha2 * (r2 + beta2 * carry_ref[2])
    residual_ref[...] = r2 - alpha2 * (carry_ref[4] + beta2 * carry_ref[3])


def small(body, rhs, shapes, *operands):
    outs = [jax.ShapeDtypeStruct(s, jnp.float32) for s in shapes]
    return pl.pallas_call(
        functools.partial(body, rhs),
        out_shape=outs,
        compiler_params=pltpu.CompilerParams(vmem_limit_bytes=VMEM_LIMIT),
    )(*operands)


def on_device(total_stars, right_side, points, star_noise):
    rhs, own = right_side.shape
    amplitude = KERNEL_WEIGHT / total_stars
    noise = star_noise[None, :]
    vector, augmented, spare = (rhs, own), (rhs + SPARE, own), (SPARE, own)
    places = jnp.concatenate([points, jnp.zeros((SPARE - 2, own), jnp.float32)], axis=0)

    row_points = gather(places, ROUNDS_B)
    gathered = gather(jnp.concatenate([right_side, places], axis=0), ROUNDS_A)
    pieces, high, low = first_product(gathered, row_points, rhs, amplitude)
    sums = scatter_sum(pieces, ROUNDS_B)
    (first,) = small(update_one, rhs, [augmented], sums, right_side, noise)

    pieces = next_product(gather(first, ROUNDS_A), high, low, rhs, amplitude)
    sums = scatter_sum(pieces, ROUNDS_B)
    third, second, scalars = small(
        update_two, rhs, [augmented, vector, spare], sums, right_side, first, noise
    )

    pieces = next_product(gather(third, ROUNDS_A), high, low, rhs, amplitude)
    sums = scatter_sum(pieces, ROUNDS_B)
    dots, carry = small(
        update_three,
        rhs,
        [spare, (6, rhs, own)],
        sums,
        right_side,
        first,
        second,
        third,
        scalars,
        noise,
    )
    return tuple(small(update_four, rhs, [vector, vector], all_sum(dots), carry))


def solution(mesh):
    placed = (P(None, AXES), P(None, AXES), P(AXES))

    def whole(right_side, points, star_noise):
        return jax.shard_map(
            functools.partial(on_device, right_side.shape[1]),
            mesh=mesh,
            in_specs=placed,
            out_specs=(P(None, AXES), P(None, AXES)),
            check_vma=False,
        )(right_side, points, star_noise)

    return whole
```

```python
import functools
import math

import jax
import jax.numpy as jnp
from jax import lax
from jax.experimental import pallas as pl
from jax.experimental.pallas import tpu as pltpu
from jax.sharding import PartitionSpec as P

QUAD_XX = 1.6
QUAD_XY = 0.5
QUAD_YY = 0.7
INVERSE_SQUARE = 25.0
KERNEL_WEIGHT = 2048.0

PX = math.sqrt(QUAD_XX * INVERSE_SQUARE)
PY = QUAD_XY * INVERSE_SQUARE / PX
QY = math.sqrt(QUAD_YY * INVERSE_SQUARE - PY * PY)

AXES = ("row", "col")
LANES = 128
SPARE = 8
TILE = 256
VMEM_LIMIT = 24 * 1024 * 1024

FIRST_A, LAST_A = ("z", (3, 2, 1)), ("y", (2, 1, 3))
ROUNDS_B = (("z", (7,)), ("x", (2, 1, 3)), ("core", (1,)))


def place(index):
    row, col = divmod(index, 16)
    y, z_lo = divmod(row, 4)
    x, rest = divmod(col, 4)
    z_hi, core = divmod(rest, 2)
    return {"x": x, "y": y, "z": z_hi * 4 + z_lo, "core": core}


def number(at):
    row = at["y"] * 4 + at["z"] % 4
    return row * 16 + at["x"] * 4 + (at["z"] // 4) * 2 + at["core"]


def exchange(value, axis, mask):
    pairs = []
    for index in range(256):
        at = place(index)
        at[axis] ^= mask
        pairs.append((index, number(at)))
    return lax.ppermute(value, AXES, pairs)


def gather(block, rounds):
    for axis, masks in rounds:
        block = jnp.concatenate([block] + [exchange(block, axis, m) for m in masks], axis=0)
    return block


def scatter_sum(blocks, rounds):
    for axis, masks in reversed(rounds):
        rows = blocks.shape[0] // (len(masks) + 1)
        total = blocks[:rows]
        for i, m in enumerate(masks):
            total = total + exchange(blocks[(i + 1) * rows : (i + 2) * rows], axis, m)
        blocks = total
    return blocks


def all_sum(block):
    copies = jnp.broadcast_to(block[None], (lax.axis_size("row"),) + block.shape)
    block = jnp.sum(lax.all_to_all(copies, "row", 0, 0), axis=0)
    for axis, masks in reversed(ROUNDS_B):
        block = block + sum(exchange(block, axis, m) for m in masks)
    return block


def split(vectors):
    high = vectors.astype(jnp.bfloat16)
    low = (vectors - high.astype(jnp.float32)).astype(jnp.bfloat16)
    return high, low


def unpack(v_ref, pair_ref, rhs):
    total = jnp.zeros((SPARE, LANES), jnp.float32)
    step = rhs + SPARE
    for b in range(v_ref.shape[0] // step):
        high, low = split(v_ref[b * step : b * step + rhs, :])
        pair_ref[:rhs, b * LANES : (b + 1) * LANES] = high
        pair_ref[rhs:, b * LANES : (b + 1) * LANES] = low
        total = total + v_ref[b * step + rhs : (b + 1) * step, :]
    return total


def emit(before_ref, out_ref, tile, product, dots, rhs):
    step = rhs + SPARE
    for piece in range(TILE // LANES):
        start = pl.multiple_of((tile * (TILE // LANES) + piece) * step, 8)
        part = product[:, piece * LANES : (piece + 1) * LANES]
        spare = dots
        if before_ref is not None:
            part = part + before_ref[pl.ds(start, rhs), :]
            spare = spare + before_ref[pl.ds(start + rhs, SPARE), :]
        out_ref[pl.ds(start, rhs), :] = part
        out_ref[pl.ds(start + rhs, SPARE), :] = spare


def first_body(rhs, amplitude, v_ref, rows_ref, before_ref, out_ref, high_ref, low_ref, pair_ref, p_ref, q_ref):
    step = rhs + SPARE
    tiles, stars, _ = high_ref.shape
    unpack(v_ref, pair_ref, rhs)
    for b in range(stars // LANES):
        spare = v_ref[b * step + rhs : (b + 1) * step, :]
        x, y = to_columns(spare, 2, LANES)
        rows = slice(b * LANES, (b + 1) * LANES)
        p_ref[rows, :] = jnp.broadcast_to(PX * x + PY * y, (LANES, LANES))
        q_ref[rows, :] = jnp.broadcast_to(QY * y, (LANES, LANES))

    def tile_step(tile, carry):
        product = jnp.zeros((rhs, TILE), jnp.float32)
        row_p, row_q = [], []
        for piece in range(TILE // LANES):
            at = pl.multiple_of((tile * (TILE // LANES) + piece) * SPARE, SPARE)
            places = rows_ref[pl.ds(at, SPARE), :]
            x, y = places[0:1, :], places[1:2, :]
            row_p.append(PX * x + PY * y)
            row_q.append(QY * y)
        for j in range(0, stars, TILE):
            pieces = []
            for p, q in zip(row_p, row_q):
                delta_p = p_ref[j : j + TILE, :] - p
                delta_q = q_ref[j : j + TILE, :] - q
                square = delta_p * delta_p + delta_q * delta_q
                distance = square * lax.rsqrt(jnp.maximum(square, 1e-30))
                pieces.append(split(jnp.exp(-distance)))
            high = jnp.concatenate([h for h, _ in pieces], axis=1)
            low = jnp.concatenate([l for _, l in pieces], axis=1)
            high_ref[tile, j : j + TILE, :] = high
            low_ref[tile, j : j + TILE, :] = low
            both = jnp.dot(pair_ref[:, j : j + TILE], high, preferred_element_type=jnp.float32)
            rest = jnp.dot(pair_ref[:rhs, j : j + TILE], low, preferred_element_type=jnp.float32)
            product = product + (both[:rhs] + (both[rhs:] + rest))
        emit(before_ref, out_ref, tile, product * amplitude, jnp.zeros((SPARE, LANES), jnp.float32), rhs)
        return carry

    lax.fori_loop(0, tiles, tile_step, 0)


def next_body(rhs, amplitude, v_ref, high_ref, low_ref, before_ref, out_ref, pair_ref):
    dots = unpack(v_ref, pair_ref, rhs)
    for tile in range(high_ref.shape[0]):
        both = jnp.dot(pair_ref[...], high_ref[tile], preferred_element_type=jnp.float32)
        rest = jnp.dot(pair_ref[:rhs, :], low_ref[tile], preferred_element_type=jnp.float32)
        product = (both[:rhs] + (both[rhs:] + rest)) * amplitude
        emit(before_ref, out_ref, tile, product, dots, rhs)


def no_before(body, at, *refs):
    body(*refs[:at], None, *refs[at:])


def kernel_call(body, outs, scratch, flops, operands):
    whole = pl.BlockSpec(memory_space=pltpu.VMEM)
    return pl.pallas_call(
        body,
        in_specs=[whole] * len(operands),
        out_specs=[whole] * len(outs),
        out_shape=outs,
        scratch_shapes=scratch,
        cost_estimate=pl.CostEstimate(flops=flops, bytes_accessed=0, transcendentals=0),
        compiler_params=pltpu.CompilerParams(vmem_limit_bytes=VMEM_LIMIT),
    )(*operands)


def first_product(part, row_points, before, rhs, amplitude):
    columns = part.shape[0] // (rhs + SPARE) * LANES
    pieces = row_points.shape[0] // SPARE
    tiles = pieces * LANES // TILE
    shape = (tiles, columns, TILE)
    outs = [
        jax.ShapeDtypeStruct((pieces * (rhs + SPARE), LANES), jnp.float32),
        jax.ShapeDtypeStruct(shape, jnp.bfloat16),
        jax.ShapeDtypeStruct(shape, jnp.bfloat16),
    ]
    scratch = [
        pltpu.VMEM((2 * rhs, columns), jnp.bfloat16),
        pltpu.VMEM((columns, LANES), jnp.float32),
        pltpu.VMEM((columns, LANES), jnp.float32),
    ]
    body = functools.partial(first_body, rhs, amplitude)
    operands = [part, row_points]
    if before is None:
        body = functools.partial(no_before, body, 2)
    else:
        operands.append(before)
    return kernel_call(body, outs, scratch, 3 << 30, operands)


def next_product(part, high, low, before, rhs, amplitude):
    tiles, columns, _ = high.shape
    outs = [
        jax.ShapeDtypeStruct((tiles * (TILE // LANES) * (rhs + SPARE), LANES), jnp.float32)
    ]
    scratch = [pltpu.VMEM((2 * rhs, columns), jnp.bfloat16)]
    body = functools.partial(next_body, rhs, amplitude)
    operands = [part, high, low]
    if before is None:
        body = functools.partial(no_before, body, 3)
    else:
        operands.append(before)
    return kernel_call(body, outs, scratch, 1 << 30, operands)[0]


def parts_of(block):
    axis, masks = LAST_A
    block = gather(block, (FIRST_A,))
    return [block] + [exchange(block, axis, m) for m in masks]


def dot(a, b):
    return jnp.sum(a * b, axis=1, keepdims=True)


def to_rows(columns, rhs):
    lane = lax.broadcasted_iota(jnp.int32, (rhs, LANES), 1)
    tile = jnp.zeros((rhs, LANES), jnp.float32)
    for i, column in enumerate(columns):
        tile = jnp.where(lane == i, column, tile)
    square = jnp.concatenate([tile, jnp.zeros((LANES - rhs, LANES), jnp.float32)], axis=0)
    return square.T[:SPARE, :]


def to_columns(tile, count, rhs):
    square = jnp.concatenate([tile, jnp.zeros((LANES - SPARE, LANES), jnp.float32)], axis=0).T
    return [square[:rhs, i : i + 1] for i in range(count)]


def pack(rhs, right_ref, points_ref, noise_ref, out_ref, places_ref):
    spare = jnp.concatenate(
        [points_ref[...], noise_ref[...], jnp.zeros((SPARE - 3, LANES), jnp.float32)], axis=0
    )
    out_ref[:rhs, :] = right_ref[...]
    out_ref[rhs:, :] = spare
    places_ref[...] = spare


def right_and_noise(packed_ref, rhs):
    return packed_ref[:rhs, :], packed_ref[rhs + 2 : rhs + 3, :]


def update_one(rhs, sums_ref, packed_ref, out_ref):
    right, noise = right_and_noise(packed_ref, rhs)
    image = sums_ref[:rhs, :] + noise * right
    out_ref[:rhs, :] = image
    out_ref[rhs:, :] = to_rows([dot(right, right), dot(right, image)], rhs)


def update_two(rhs, sums_ref, packed_ref, first_ref, out_ref, second_ref, scalars_ref):
    right, noise = right_and_noise(packed_ref, rhs)
    w0 = first_ref[:rhs, :]
    n0 = sums_ref[:rhs, :] + noise * w0
    norm, curve = to_columns(sums_ref[rhs:, :], 2, rhs)
    alpha = norm / curve
    r1 = right - alpha * w0
    w1 = w0 - alpha * n0
    out_ref[:rhs, :] = w1
    out_ref[rhs:, :] = to_rows([dot(r1, r1), dot(r1, w1)], rhs)
    second_ref[...] = n0
    scalars_ref[...] = sums_ref[rhs:, :]


def update_three(rhs, sums_ref, packed_ref, first_ref, second_ref, third_ref, scalars_ref, dots_ref, carry_ref):
    right, noise = right_and_noise(packed_ref, rhs)
    w0 = first_ref[:rhs, :]
    n0 = second_ref[...]
    w1 = third_ref[:rhs, :]
    n1 = sums_ref[:rhs, :] + noise * w1
    norm0, curve0 = to_columns(scalars_ref[...], 2, rhs)
    norm1, curve1 = to_columns(sums_ref[rhs:, :], 2, rhs)
    alpha0 = norm0 / curve0
    beta1 = norm1 / norm0
    alpha1 = norm1 / (curve1 - beta1 * norm1 / alpha0)
    r1 = right - alpha0 * w0
    s1 = w1 + beta1 * w0
    p1 = r1 + beta1 * right
    z1 = n1 + beta1 * n0
    r2 = r1 - alpha1 * s1
    w2 = w1 - alpha1 * z1
    dots_ref[...] = to_rows([dot(r2, r2), dot(r2, w2)], rhs)
    lane = lax.broadcasted_iota(jnp.int32, (rhs, LANES), 1)
    carry_ref[0] = alpha0 * right + alpha1 * p1
    carry_ref[1] = r2
    carry_ref[2] = p1
    carry_ref[3] = s1
    carry_ref[4] = w2
    carry_ref[5] = jnp.where(lane == 0, alpha1, norm1)


def update_four(rhs, dots_ref, carry_ref, solution_ref, residual_ref):
    norm2, curve2 = to_columns(dots_ref[...], 2, rhs)
    alpha1 = carry_ref[5, :, 0:1]
    norm1 = carry_ref[5, :, 1:2]
    r2 = carry_ref[1]
    beta2 = norm2 / norm1
    alpha2 = norm2 / (curve2 - beta2 * norm2 / alpha1)
    solution_ref[...] = carry_ref[0] + alpha2 * (r2 + beta2 * carry_ref[2])
    residual_ref[...] = r2 - alpha2 * (carry_ref[4] + beta2 * carry_ref[3])


def small(body, rhs, shapes, *operands):
    outs = [jax.ShapeDtypeStruct(s, jnp.float32) for s in shapes]
    return pl.pallas_call(
        functools.partial(body, rhs),
        out_shape=outs,
        compiler_params=pltpu.CompilerParams(vmem_limit_bytes=VMEM_LIMIT),
    )(*operands)


def on_device(total_stars, right_side, points, star_noise):
    rhs, own = right_side.shape
    amplitude = KERNEL_WEIGHT / total_stars
    vector, augmented, spare = (rhs, own), (rhs + SPARE, own), (SPARE, own)

    packed, places = small(
        pack, rhs, [augmented, spare], right_side, points, star_noise[None, :]
    )
    row_points = gather(places, ROUNDS_B)
    pieces, kernel = None, []
    for part in parts_of(packed):
        pieces, high, low = first_product(part, row_points, pieces, rhs, amplitude)
        kernel.append((high, low))
    sums = scatter_sum(pieces, ROUNDS_B)
    (first,) = small(update_one, rhs, [augmented], sums, packed)

    def product(block):
        pieces = None
        for part, (high, low) in zip(parts_of(block), kernel):
            pieces = next_product(part, high, low, pieces, rhs, amplitude)
        return scatter_sum(pieces, ROUNDS_B)

    third, second, scalars = small(
        update_two, rhs, [augmented, vector, spare], product(first), packed, first
    )
    dots, carry = small(
        update_three,
        rhs,
        [spare, (6, rhs, own)],
        product(third),
        packed,
        first,
        second,
        third,
        scalars,
    )
    return tuple(small(update_four, rhs, [vector, vector], all_sum(dots), carry))


def solution(mesh):
    placed = (P(None, AXES), P(None, AXES), P(AXES))

    def whole(right_side, points, star_noise):
        return jax.shard_map(
            functools.partial(on_device, right_side.shape[1]),
            mesh=mesh,
            in_specs=placed,
            out_specs=(P(None, AXES), P(None, AXES)),
            check_vma=False,
        )(right_side, points, star_noise)

    return whole
```

```python
import functools
import math

import jax
import jax.numpy as jnp
from jax import lax
from jax.experimental import pallas as pl
from jax.experimental.pallas import tpu as pltpu
from jax.sharding import PartitionSpec as P

QUAD_XX = 1.6
QUAD_XY = 0.5
QUAD_YY = 0.7
INVERSE_SQUARE = 25.0
KERNEL_WEIGHT = 2048.0

LOG2E = math.log2(math.e)
PX = math.sqrt(QUAD_XX * INVERSE_SQUARE)
PY = QUAD_XY * INVERSE_SQUARE / PX
QY = math.sqrt(QUAD_YY * INVERSE_SQUARE - PY * PY)
PX, PY, QY = PX * LOG2E, PY * LOG2E, QY * LOG2E

AXES = ("row", "col")
DEVICES = 256
LANES = 128
SPARE = 8
TILE = 256
VMEM_LIMIT = 24 * 1024 * 1024


def place(index):
    row, col = divmod(index, 16)
    y, z_lo = divmod(row, 4)
    x, rest = divmod(col, 4)
    z_hi, core = divmod(rest, 2)
    return {"x": x, "y": y, "z": z_hi * 4 + z_lo, "core": core}


def number(at):
    row = at["y"] * 4 + at["z"] % 4
    return row * 16 + at["x"] * 4 + (at["z"] // 4) * 2 + at["core"]


def groups_along(*axes):
    groups = {}
    for index in range(DEVICES):
        rest = tuple(v for k, v in place(index).items() if k not in axes)
        groups.setdefault(rest, []).append(index)
    return list(groups.values())


PLANES = groups_along("x", "y")
COLUMNS = groups_along("z", "core")


def exchange(value, axis, mask):
    pairs = []
    for index in range(DEVICES):
        at = place(index)
        at[axis] ^= mask
        pairs.append((index, number(at)))
    return lax.ppermute(value, AXES, pairs)


def parts_of(block):
    near = jnp.concatenate([block] + [exchange(block, "z", m) for m in (3, 2, 1)], axis=0)
    far = exchange(near, "z", 7)
    return [near, exchange(near, "core", 1), far, exchange(far, "core", 1)]


def deal(blocks, groups):
    count = len(groups[0])
    rows = blocks.shape[0] // count
    dealt = lax.all_to_all(
        blocks.reshape(count, rows, LANES), AXES, 0, 0, axis_index_groups=groups
    )
    return dealt.reshape(count * rows, LANES)


def all_sum(block):
    for groups in (COLUMNS, PLANES):
        copies = jnp.broadcast_to(block[None], (len(groups[0]),) + block.shape)
        dealt = lax.all_to_all(copies, AXES, 0, 0, axis_index_groups=groups)
        block = jnp.sum(dealt, axis=0)
    return block


def split(vectors):
    high = vectors.astype(jnp.bfloat16)
    low = (vectors - high.astype(jnp.float32)).astype(jnp.bfloat16)
    return high, low


def as_columns(row, rhs):
    return jnp.broadcast_to(row, (LANES, LANES)).T[:rhs, :]


def unpack(v_ref, pair_ref, rhs):
    total = jnp.zeros((SPARE, LANES), jnp.float32)
    step = rhs + SPARE
    for b in range(v_ref.shape[0] // step):
        high, low = split(v_ref[b * step : b * step + rhs, :])
        pair_ref[:rhs, b * LANES : (b + 1) * LANES] = high
        pair_ref[rhs:, b * LANES : (b + 1) * LANES] = low
        total = total + v_ref[b * step + rhs : (b + 1) * step, :]
    return total


def emit(before_ref, out_ref, tile, product, dots, rhs):
    step = rhs + SPARE
    for piece in range(TILE // LANES):
        start = (tile * (TILE // LANES) + piece) * step
        part = product[:, piece * LANES : (piece + 1) * LANES]
        spare = dots
        if before_ref is not None:
            part = part + before_ref[start : start + rhs, :]
            spare = spare + before_ref[start + rhs : start + step, :]
        out_ref[start : start + rhs, :] = part
        out_ref[start + rhs : start + step, :] = spare


def first_body(rhs, amplitude, v_ref, rows_ref, before_ref, out_ref, high_ref, low_ref, pair_ref, p_ref, q_ref):
    step = rhs + SPARE
    tiles, stars, _ = high_ref.shape
    unpack(v_ref, pair_ref, rhs)
    for b in range(stars // LANES):
        x = v_ref[b * step + rhs : b * step + rhs + 1, :]
        y = v_ref[b * step + rhs + 1 : b * step + rhs + 2, :]
        rows = slice(b * LANES, (b + 1) * LANES)
        p_ref[rows, :] = as_columns(PX * x + PY * y, LANES)
        q_ref[rows, :] = as_columns(QY * y, LANES)

    for tile in range(tiles):
        product = jnp.zeros((rhs, TILE), jnp.float32)
        for j in range(0, stars, TILE):
            pieces = []
            for piece in range(TILE // LANES):
                at = (tile * (TILE // LANES) + piece) * SPARE
                x, y = rows_ref[at : at + 1, :], rows_ref[at + 1 : at + 2, :]
                delta_p = p_ref[j : j + TILE, :] - (PX * x + PY * y)
                delta_q = q_ref[j : j + TILE, :] - QY * y
                square = delta_p * delta_p + delta_q * delta_q
                distance = square * lax.rsqrt(jnp.maximum(square, 1e-30))
                pieces.append(split(jnp.exp2(-distance)))
            high = jnp.concatenate([h for h, _ in pieces], axis=1)
            low = jnp.concatenate([l for _, l in pieces], axis=1)
            high_ref[tile, j : j + TILE, :] = high
            low_ref[tile, j : j + TILE, :] = low
            both = jnp.dot(pair_ref[:, j : j + TILE], high, preferred_element_type=jnp.float32)
            rest = jnp.dot(pair_ref[:rhs, j : j + TILE], low, preferred_element_type=jnp.float32)
            product = product + (both[:rhs] + (both[rhs:] + rest))
        emit(before_ref, out_ref, tile, product * amplitude, jnp.zeros((SPARE, LANES), jnp.float32), rhs)


def next_body(rhs, amplitude, v_ref, high_ref, low_ref, before_ref, out_ref, pair_ref):
    dots = unpack(v_ref, pair_ref, rhs)
    for tile in range(high_ref.shape[0]):
        both = jnp.dot(pair_ref[...], high_ref[tile], preferred_element_type=jnp.float32)
        rest = jnp.dot(pair_ref[:rhs, :], low_ref[tile], preferred_element_type=jnp.float32)
        product = (both[:rhs] + (both[rhs:] + rest)) * amplitude
        emit(before_ref, out_ref, tile, product, dots, rhs)


def no_before(body, at, *refs):
    body(*refs[:at], None, *refs[at:])


def kernel_call(body, outs, scratch, flops, operands):
    whole = pl.BlockSpec(memory_space=pltpu.VMEM)
    return pl.pallas_call(
        body,
        in_specs=[whole] * len(operands),
        out_specs=[whole] * len(outs),
        out_shape=outs,
        scratch_shapes=scratch,
        cost_estimate=pl.CostEstimate(flops=flops, bytes_accessed=0, transcendentals=0),
        compiler_params=pltpu.CompilerParams(vmem_limit_bytes=VMEM_LIMIT),
    )(*operands)


def first_product(part, row_points, before, rhs, amplitude):
    columns = part.shape[0] // (rhs + SPARE) * LANES
    pieces = row_points.shape[0] // SPARE
    tiles = pieces * LANES // TILE
    shape = (tiles, columns, TILE)
    outs = [
        jax.ShapeDtypeStruct((pieces * (rhs + SPARE), LANES), jnp.float32),
        jax.ShapeDtypeStruct(shape, jnp.bfloat16),
        jax.ShapeDtypeStruct(shape, jnp.bfloat16),
    ]
    scratch = [
        pltpu.VMEM((2 * rhs, columns), jnp.bfloat16),
        pltpu.VMEM((columns, LANES), jnp.float32),
        pltpu.VMEM((columns, LANES), jnp.float32),
    ]
    body = functools.partial(first_body, rhs, amplitude)
    operands = [part, row_points]
    if before is None:
        body = functools.partial(no_before, body, 2)
    else:
        operands.append(before)
    return kernel_call(body, outs, scratch, 3 << 30, operands)


def next_product(part, high, low, before, rhs, amplitude):
    tiles, columns, _ = high.shape
    outs = [
        jax.ShapeDtypeStruct((tiles * (TILE // LANES) * (rhs + SPARE), LANES), jnp.float32)
    ]
    scratch = [pltpu.VMEM((2 * rhs, columns), jnp.bfloat16)]
    body = functools.partial(next_body, rhs, amplitude)
    operands = [part, high, low]
    if before is None:
        body = functools.partial(no_before, body, 3)
    else:
        operands.append(before)
    return kernel_call(body, outs, scratch, 1 << 30, operands)[0]


def dot(a, b):
    return jnp.sum(a * b, axis=1, keepdims=True)


def to_rows(columns, rhs):
    lane = lax.broadcasted_iota(jnp.int32, (rhs, LANES), 1)
    tile = jnp.zeros((rhs, LANES), jnp.float32)
    for i, column in enumerate(columns):
        tile = jnp.where(lane == i, column, tile)
    square = jnp.concatenate([tile, jnp.zeros((LANES - rhs, LANES), jnp.float32)], axis=0)
    return square.T[:SPARE, :]


def pack(rhs, right_ref, points_ref, noise_ref, out_ref, places_ref):
    spare = jnp.concatenate(
        [points_ref[...], noise_ref[...], jnp.zeros((SPARE - 3, LANES), jnp.float32)], axis=0
    )
    out_ref[:rhs, :] = right_ref[...]
    out_ref[rhs:, :] = spare
    for copy in range(places_ref.shape[0] // SPARE):
        places_ref[copy * SPARE : (copy + 1) * SPARE, :] = spare


def summed(dealt_ref, rhs):
    step = rhs + SPARE
    blocks = [dealt_ref[at : at + step, :] for at in range(0, dealt_ref.shape[0], step)]
    while len(blocks) > 1:
        blocks = [a + b for a, b in zip(blocks[::2], blocks[1::2])]
    return blocks[0][:rhs, :], blocks[0][rhs:, :]


def right_and_noise(packed_ref, rhs):
    return packed_ref[:rhs, :], packed_ref[rhs + 2 : rhs + 3, :]


def update_one(rhs, dealt_ref, packed_ref, out_ref):
    right, noise = right_and_noise(packed_ref, rhs)
    image, _ = summed(dealt_ref, rhs)
    image = image + noise * right
    out_ref[:rhs, :] = image
    out_ref[rhs:, :] = to_rows([dot(right, right), dot(right, image)], rhs)


def update_two(rhs, dealt_ref, packed_ref, first_ref, out_ref, second_ref, scalars_ref):
    right, noise = right_and_noise(packed_ref, rhs)
    w0 = first_ref[:rhs, :]
    image, dots = summed(dealt_ref, rhs)
    n0 = image + noise * w0
    alpha = as_columns(dots[0:1, :] / dots[1:2, :], rhs)
    r1 = right - alpha * w0
    w1 = w0 - alpha * n0
    out_ref[:rhs, :] = w1
    out_ref[rhs:, :] = to_rows([dot(r1, r1), dot(r1, w1)], rhs)
    second_ref[...] = n0
    scalars_ref[...] = dots


def update_three(rhs, dealt_ref, packed_ref, first_ref, second_ref, third_ref, scalars_ref, dots_ref, carry_ref, kept_ref):
    right, noise = right_and_noise(packed_ref, rhs)
    w0 = first_ref[:rhs, :]
    n0 = second_ref[...]
    w1 = third_ref[:rhs, :]
    image, dots = summed(dealt_ref, rhs)
    n1 = image + noise * w1
    norm0, curve0 = scalars_ref[0:1, :], scalars_ref[1:2, :]
    norm1, curve1 = dots[0:1, :], dots[1:2, :]
    alpha0_row = norm0 / curve0
    beta1_row = norm1 / norm0
    alpha1_row = norm1 / (curve1 - beta1_row * norm1 / alpha0_row)
    alpha0, beta1, alpha1 = (as_columns(row, rhs) for row in (alpha0_row, beta1_row, alpha1_row))
    r1 = right - alpha0 * w0
    s1 = w1 + beta1 * w0
    p1 = r1 + beta1 * right
    z1 = n1 + beta1 * n0
    r2 = r1 - alpha1 * s1
    w2 = w1 - alpha1 * z1
    dots_ref[...] = to_rows([dot(r2, r2), dot(r2, w2)], rhs)
    carry_ref[0] = alpha0 * right + alpha1 * p1
    carry_ref[1] = r2
    carry_ref[2] = p1
    carry_ref[3] = s1
    carry_ref[4] = w2
    kept_ref[...] = jnp.concatenate(
        [norm1, alpha1_row, jnp.zeros((SPARE - 2, LANES), jnp.float32)], axis=0
    )


def update_four(rhs, dots_ref, carry_ref, kept_ref, solution_ref, residual_ref):
    norm2, curve2 = dots_ref[0:1, :], dots_ref[1:2, :]
    norm1, alpha1 = kept_ref[0:1, :], kept_ref[1:2, :]
    beta2_row = norm2 / norm1
    alpha2 = as_columns(norm2 / (curve2 - beta2_row * norm2 / alpha1), rhs)
    beta2 = as_columns(beta2_row, rhs)
    r2 = carry_ref[1]
    solution_ref[...] = carry_ref[0] + alpha2 * (r2 + beta2 * carry_ref[2])
    residual_ref[...] = r2 - alpha2 * (carry_ref[4] + beta2 * carry_ref[3])


def small(body, rhs, shapes, *operands):
    outs = [jax.ShapeDtypeStruct(s, jnp.float32) for s in shapes]
    return pl.pallas_call(
        functools.partial(body, rhs),
        out_shape=outs,
        compiler_params=pltpu.CompilerParams(vmem_limit_bytes=VMEM_LIMIT),
    )(*operands)


def on_device(total_stars, right_side, points, star_noise):
    rhs, own = right_side.shape
    amplitude = KERNEL_WEIGHT / total_stars
    vector, augmented, spare = (rhs, own), (rhs + SPARE, own), (SPARE, own)

    packed, places = small(
        pack,
        rhs,
        [augmented, (SPARE * len(PLANES[0]), own)],
        right_side,
        points,
        star_noise[None, :],
    )
    row_points = deal(places, PLANES)
    pieces, kernel = None, []
    for part in parts_of(packed):
        pieces, high, low = first_product(part, row_points, pieces, rhs, amplitude)
        kernel.append((high, low))
    (first,) = small(update_one, rhs, [augmented], deal(pieces, PLANES), packed)

    def product(block):
        pieces = None
        for part, (high, low) in zip(parts_of(block), kernel):
            pieces = next_product(part, high, low, pieces, rhs, amplitude)
        return deal(pieces, PLANES)

    third, second, scalars = small(
        update_two, rhs, [augmented, vector, spare], product(first), packed, first
    )
    dots, carry, kept = small(
        update_three,
        rhs,
        [spare, (5, rhs, own), spare],
        product(third),
        packed,
        first,
        second,
        third,
        scalars,
    )
    return tuple(small(update_four, rhs, [vector, vector], all_sum(dots), carry, kept))


def solution(mesh):
    placed = (P(None, AXES), P(None, AXES), P(AXES))

    def whole(right_side, points, star_noise):
        return jax.shard_map(
            functools.partial(on_device, right_side.shape[1]),
            mesh=mesh,
            in_specs=placed,
            out_specs=(P(None, AXES), P(None, AXES)),
            check_vma=False,
        )(right_side, points, star_noise)

    return whole
```

```python
import functools
import math

import jax
import jax.numpy as jnp
from jax import lax
from jax.experimental import pallas as pl
from jax.experimental.pallas import tpu as pltpu
from jax.sharding import PartitionSpec as P

QUAD_XX = 1.6
QUAD_XY = 0.5
QUAD_YY = 0.7
INVERSE_SQUARE = 25.0
KERNEL_WEIGHT = 2048.0

LOG2E = math.log2(math.e)
PX = math.sqrt(QUAD_XX * INVERSE_SQUARE)
PY = QUAD_XY * INVERSE_SQUARE / PX
QY = math.sqrt(QUAD_YY * INVERSE_SQUARE - PY * PY)
PX, PY, QY = PX * LOG2E, PY * LOG2E, QY * LOG2E

AXES = ("row", "col")
DEVICES = 256
LANES = 128
SPARE = 8
TILE = 256
VMEM_LIMIT = 24 * 1024 * 1024


def place(index):
    row, col = divmod(index, 16)
    y, z_lo = divmod(row, 4)
    x, rest = divmod(col, 4)
    z_hi, core = divmod(rest, 2)
    return {"x": x, "y": y, "z": z_hi * 4 + z_lo, "core": core}


def number(at):
    row = at["y"] * 4 + at["z"] % 4
    return row * 16 + at["x"] * 4 + (at["z"] // 4) * 2 + at["core"]


def groups_along(*axes):
    groups = {}
    for index in range(DEVICES):
        rest = tuple(v for k, v in place(index).items() if k not in axes)
        groups.setdefault(rest, []).append(index)
    return list(groups.values())


PLANES = groups_along("x", "y")
LINES = groups_along("z")
COLUMNS = groups_along("z", "core")
NEAR = (3, 2, 1)
BLOCKS = (0,) + NEAR + tuple(7 ^ m for m in (0,) + NEAR)


def exchange(value, axis, mask):
    pairs = []
    for index in range(DEVICES):
        at = place(index)
        at[axis] ^= mask
        pairs.append((index, number(at)))
    return lax.ppermute(value, AXES, pairs)


def parts_of(block):
    near = jnp.concatenate([block] + [exchange(block, "z", m) for m in NEAR], axis=0)
    far = exchange(near, "z", 7)
    return [near, exchange(near, "core", 1), far, exchange(far, "core", 1)]


def deal(blocks, groups):
    count = len(groups[0])
    rows = blocks.shape[0] // count
    dealt = lax.all_to_all(
        blocks.reshape(count, rows, LANES), AXES, 0, 0, axis_index_groups=groups
    )
    return dealt.reshape(count * rows, LANES)


def all_sum(block):
    for groups in (PLANES, COLUMNS):
        copies = jnp.broadcast_to(block[None], (len(groups[0]),) + block.shape)
        dealt = lax.all_to_all(copies, AXES, 0, 0, axis_index_groups=groups)
        block = jnp.sum(dealt, axis=0)
    return block


def split(vectors):
    high = vectors.astype(jnp.bfloat16)
    low = (vectors - high.astype(jnp.float32)).astype(jnp.bfloat16)
    return high, low


def as_columns(row, rhs):
    return jnp.broadcast_to(row, (LANES, LANES)).T[:rhs, :]


def put_pair(pair_ref, b, block, rhs):
    high, low = split(block)
    pair_ref[:rhs, b * LANES : (b + 1) * LANES] = high
    pair_ref[rhs:, b * LANES : (b + 1) * LANES] = low


def first_body(rhs, amplitude, has_before, v_ref, rows_ref, *refs):
    before_ref, refs = (refs[0], refs[1:]) if has_before else (None, refs)
    out_ref, high_ref, low_ref, pair_ref, p_ref, q_ref = refs
    step = rhs + SPARE
    tiles, stars, _ = high_ref.shape
    for b in range(stars // LANES):
        at = b * step + rhs
        put_pair(pair_ref, b, v_ref[at - rhs : at, :], rhs)
        x, y = v_ref[at : at + 1, :], v_ref[at + 1 : at + 2, :]
        rows = slice(b * LANES, (b + 1) * LANES)
        p_ref[rows, :] = as_columns(PX * x + PY * y, LANES)
        q_ref[rows, :] = as_columns(QY * y, LANES)

    for tile in range(tiles):
        product = jnp.zeros((rhs, TILE), jnp.float32)
        for j in range(0, stars, TILE):
            pieces = []
            for piece in range(TILE // LANES):
                at = (tile * (TILE // LANES) + piece) * SPARE
                x, y = rows_ref[at : at + 1, :], rows_ref[at + 1 : at + 2, :]
                delta_p = p_ref[j : j + TILE, :] - (PX * x + PY * y)
                delta_q = q_ref[j : j + TILE, :] - QY * y
                square = delta_p * delta_p + delta_q * delta_q
                distance = square * lax.rsqrt(jnp.maximum(square, 1e-30))
                pieces.append(split(jnp.exp2(-distance)))
            high = jnp.concatenate([h for h, _ in pieces], axis=1)
            low = jnp.concatenate([l for _, l in pieces], axis=1)
            high_ref[tile, j : j + TILE, :] = high
            low_ref[tile, j : j + TILE, :] = low
            both = jnp.dot(pair_ref[:, j : j + TILE], high, preferred_element_type=jnp.float32)
            rest = jnp.dot(pair_ref[:rhs, j : j + TILE], low, preferred_element_type=jnp.float32)
            product = product + (both[:rhs] + (both[rhs:] + rest))
        for piece in range(TILE // LANES):
            at = (tile * (TILE // LANES) + piece) * rhs
            part = product[:, piece * LANES : (piece + 1) * LANES] * amplitude
            if has_before:
                part = part + before_ref[at : at + rhs, :]
            out_ref[at : at + rhs, :] = part


def next_body(rhs, amplitude, has_last, has_before, v_ref, right_near_ref, right_far_ref, *refs):
    last_ref, scalars_ref, refs = (refs[0], refs[1], refs[2:]) if has_last else (None, None, refs)
    before_ref, refs = (refs[0], refs[1:]) if has_before else (None, refs)
    kernel, out_ref, pair_ref = refs[:4], refs[4], refs[5]
    step = rhs + SPARE
    z_lo = lax.rem(lax.axis_index("row"), 4)
    z_hi = lax.rem(lax.div(lax.axis_index("col"), 2), 2)
    if has_last:
        alpha = as_columns(scalars_ref[0:1, :] / scalars_ref[1:2, :], rhs)
    norm = jnp.zeros((rhs, LANES), jnp.float32)
    curve = jnp.zeros((rhs, LANES), jnp.float32)
    half = len(BLOCKS) // 2
    for b, mask in enumerate(BLOCKS):
        lo, hi = lax.bitwise_xor(z_lo, mask % 4), lax.bitwise_xor(z_hi, mask // 4)
        at = pl.multiple_of((lo * 2 + hi) * rhs, rhs)
        block = v_ref[pl.ds(at, rhs), :]
        put_pair(pair_ref, b, block, rhs)
        right_ref = right_near_ref if b < half else right_far_ref
        residual = right_ref[b % half * step : b % half * step + rhs, :]
        if has_last:
            residual = residual - alpha * last_ref[pl.ds(at, rhs), :]
        norm = norm + residual * residual
        curve = curve + residual * block
    ones = jnp.ones((rhs, LANES), jnp.float32)
    dots = to_rows([dot(norm, ones), dot(curve, ones)], rhs)
    if has_before:
        dots = dots + before_ref[rhs:step, :]

    columns = half * LANES
    for tile in range(kernel[0].shape[0]):
        product = jnp.zeros((rhs, TILE), jnp.float32)
        for part in range(2):
            cut = slice(part * columns, (part + 1) * columns)
            high, low = kernel[2 * part][tile], kernel[2 * part + 1][tile]
            both = jnp.dot(pair_ref[:, cut], high, preferred_element_type=jnp.float32)
            rest = jnp.dot(pair_ref[:rhs, cut], low, preferred_element_type=jnp.float32)
            product = product + (both[:rhs] + (both[rhs:] + rest))
        for piece in range(TILE // LANES):
            at = (tile * (TILE // LANES) + piece) * step
            part = product[:, piece * LANES : (piece + 1) * LANES] * amplitude
            if has_before:
                part = part + before_ref[at : at + rhs, :]
            out_ref[at : at + rhs, :] = part
            out_ref[at + rhs : at + step, :] = dots


def kernel_call(body, outs, scratch, flops, operands):
    whole = pl.BlockSpec(memory_space=pltpu.VMEM)
    return pl.pallas_call(
        body,
        in_specs=[whole] * len(operands),
        out_specs=[whole] * len(outs),
        out_shape=outs,
        scratch_shapes=scratch,
        cost_estimate=pl.CostEstimate(flops=flops, bytes_accessed=0, transcendentals=0),
        compiler_params=pltpu.CompilerParams(vmem_limit_bytes=VMEM_LIMIT),
    )(*operands)


def first_product(part, row_points, before, rhs, amplitude):
    columns = part.shape[0] // (rhs + SPARE) * LANES
    pieces = row_points.shape[0] // SPARE
    shape = (pieces * LANES // TILE, columns, TILE)
    outs = [
        jax.ShapeDtypeStruct((pieces * rhs, LANES), jnp.float32),
        jax.ShapeDtypeStruct(shape, jnp.bfloat16),
        jax.ShapeDtypeStruct(shape, jnp.bfloat16),
    ]
    scratch = [
        pltpu.VMEM((2 * rhs, columns), jnp.bfloat16),
        pltpu.VMEM((columns, LANES), jnp.float32),
        pltpu.VMEM((columns, LANES), jnp.float32),
    ]
    operands = [part, row_points] + ([] if before is None else [before])
    body = functools.partial(first_body, rhs, amplitude, before is not None)
    return kernel_call(body, outs, scratch, 3 << 30, operands)


def next_product(vectors, rights, last, scalars, before, kernels, rhs, amplitude):
    tiles, columns, _ = kernels[0][0].shape
    rows = tiles * (TILE // LANES) * (rhs + SPARE)
    outs = [jax.ShapeDtypeStruct((rows, LANES), jnp.float32)]
    scratch = [pltpu.VMEM((2 * rhs, 2 * columns), jnp.bfloat16)]
    operands = [vectors, *rights]
    operands += [] if last is None else [last, scalars]
    operands += [] if before is None else [before]
    operands += [half for kernel in kernels for half in kernel]
    body = functools.partial(next_body, rhs, amplitude, last is not None, before is not None)
    return kernel_call(body, outs, scratch, 1 << 31, operands)[0]


def dot(a, b):
    return jnp.sum(a * b, axis=1, keepdims=True)


def to_rows(columns, rhs):
    lane = lax.broadcasted_iota(jnp.int32, (rhs, LANES), 1)
    tile = jnp.zeros((rhs, LANES), jnp.float32)
    for i, column in enumerate(columns):
        tile = jnp.where(lane == i, column, tile)
    square = jnp.concatenate([tile, jnp.zeros((LANES - rhs, LANES), jnp.float32)], axis=0)
    return square.T[:SPARE, :]


def pack(rhs, right_ref, points_ref, noise_ref, out_ref, places_ref, spare_ref, semaphores):
    spare_ref[...] = jnp.zeros_like(spare_ref)
    copies = [
        pltpu.make_async_copy(right_ref, out_ref.at[pl.ds(0, rhs), :], semaphores.at[0]),
        pltpu.make_async_copy(points_ref, spare_ref.at[pl.ds(0, 2), :], semaphores.at[1]),
        pltpu.make_async_copy(noise_ref, spare_ref.at[pl.ds(2, 1), :], semaphores.at[2]),
    ]
    for copy in copies:
        copy.start()
    for copy in copies:
        copy.wait()
    spare = spare_ref[...]
    out_ref[rhs:, :] = spare
    for at in range(0, places_ref.shape[0], SPARE):
        places_ref[at : at + SPARE, :] = spare


def packed_inputs(right_side, points, noise):
    rhs, own = right_side.shape
    anywhere, whole = pl.BlockSpec(memory_space=pl.ANY), pl.BlockSpec(memory_space=pltpu.VMEM)
    return pl.pallas_call(
        functools.partial(pack, rhs),
        in_specs=[anywhere] * 3,
        out_specs=[whole] * 2,
        out_shape=[
            jax.ShapeDtypeStruct((rhs + SPARE, own), jnp.float32),
            jax.ShapeDtypeStruct((SPARE * len(PLANES[0]), own), jnp.float32),
        ],
        scratch_shapes=[pltpu.VMEM((SPARE, own), jnp.float32), pltpu.SemaphoreType.DMA((3,))],
        compiler_params=pltpu.CompilerParams(vmem_limit_bytes=60 * 1024 * 1024),
    )(right_side, points, noise)


def summed(dealt_ref, step):
    blocks = [dealt_ref[at : at + step, :] for at in range(0, dealt_ref.shape[0], step)]
    while len(blocks) > 1:
        blocks = [a + b for a, b in zip(blocks[::2], blocks[1::2])]
    return blocks[0]


def right_and_noise(packed_ref, rhs):
    return packed_ref[:rhs, :], packed_ref[rhs + 2 : rhs + 3, :]


def copy_out(copies_ref, vectors):
    rows = vectors.shape[0]
    for at in range(0, copies_ref.shape[0], rows):
        copies_ref[at : at + rows, :] = vectors


def update_one(rhs, dealt_ref, packed_ref, copies_ref):
    right, noise = right_and_noise(packed_ref, rhs)
    copy_out(copies_ref, summed(dealt_ref, rhs) + noise * right)


def update_two(rhs, dealt_ref, packed_ref, first_ref, copies_ref, second_ref, scalars_ref):
    right, noise = right_and_noise(packed_ref, rhs)
    w0 = first_ref[:rhs, :]
    image = summed(dealt_ref, rhs + SPARE)
    dots = image[rhs:, :]
    n0 = image[:rhs, :] + noise * w0
    alpha = as_columns(dots[0:1, :] / dots[1:2, :], rhs)
    copy_out(copies_ref, w0 - alpha * n0)
    second_ref[...] = n0
    scalars_ref[...] = dots


def update_three(rhs, dealt_ref, packed_ref, first_ref, second_ref, third_ref, scalars_ref, dots_ref, carry_ref, kept_ref):
    right, noise = right_and_noise(packed_ref, rhs)
    w0 = first_ref[:rhs, :]
    n0 = second_ref[...]
    w1 = third_ref[:rhs, :]
    image = summed(dealt_ref, rhs + SPARE)
    dots = image[rhs:, :]
    n1 = image[:rhs, :] + noise * w1
    norm0, curve0 = scalars_ref[0:1, :], scalars_ref[1:2, :]
    norm1, curve1 = dots[0:1, :], dots[1:2, :]
    alpha0_row = norm0 / curve0
    beta1_row = norm1 / norm0
    alpha1_row = norm1 / (curve1 - beta1_row * norm1 / alpha0_row)
    alpha0, beta1, alpha1 = (as_columns(row, rhs) for row in (alpha0_row, beta1_row, alpha1_row))
    r1 = right - alpha0 * w0
    s1 = w1 + beta1 * w0
    p1 = r1 + beta1 * right
    z1 = n1 + beta1 * n0
    r2 = r1 - alpha1 * s1
    w2 = w1 - alpha1 * z1
    dots_ref[...] = to_rows([dot(r2, r2), dot(r2, w2)], rhs)
    carry_ref[0] = alpha0 * right + alpha1 * p1
    carry_ref[1] = r2
    carry_ref[2] = p1
    carry_ref[3] = s1
    carry_ref[4] = w2
    kept_ref[...] = jnp.concatenate(
        [norm1, alpha1_row, jnp.zeros((SPARE - 2, LANES), jnp.float32)], axis=0
    )


def update_four(rhs, dots_ref, carry_ref, kept_ref, solution_ref, residual_ref):
    norm2, curve2 = dots_ref[0:1, :], dots_ref[1:2, :]
    norm1, alpha1 = kept_ref[0:1, :], kept_ref[1:2, :]
    beta2_row = norm2 / norm1
    alpha2 = as_columns(norm2 / (curve2 - beta2_row * norm2 / alpha1), rhs)
    beta2 = as_columns(beta2_row, rhs)
    r2 = carry_ref[1]
    solution_ref[...] = carry_ref[0] + alpha2 * (r2 + beta2 * carry_ref[2])
    residual_ref[...] = r2 - alpha2 * (carry_ref[4] + beta2 * carry_ref[3])


def small(body, rhs, shapes, *operands):
    outs = [jax.ShapeDtypeStruct(s, jnp.float32) for s in shapes]
    return pl.pallas_call(
        functools.partial(body, rhs),
        out_shape=outs,
        compiler_params=pltpu.CompilerParams(vmem_limit_bytes=VMEM_LIMIT),
    )(*operands)


def on_device(total_stars, right_side, points, star_noise):
    rhs, own = right_side.shape
    amplitude = KERNEL_WEIGHT / total_stars
    vector, spare, copies = (rhs, own), (SPARE, own), (rhs * len(BLOCKS), own)

    packed, places = packed_inputs(right_side, points, star_noise[None, :])
    row_points = deal(places, PLANES)
    rights = parts_of(packed)
    pieces, kernels = None, []
    for part in rights:
        pieces, high, low = first_product(part, row_points, pieces, rhs, amplitude)
        kernels.append((high, low))
    (first,) = small(update_one, rhs, [copies], deal(pieces, PLANES), packed)

    def product(vectors, lasts, scalars):
        mine = deal(vectors, LINES)
        other = exchange(mine, "core", 1)
        pieces = None
        for n, part in enumerate((mine, other)):
            pieces = next_product(
                part, rights[n::2], lasts[n], scalars, pieces, kernels[n::2], rhs, amplitude
            )
        return deal(pieces, PLANES), (mine, other)

    dealt, gathered = product(first, (None, None), None)
    third, second, scalars = small(
        update_two, rhs, [copies, vector, spare], dealt, packed, first
    )
    dealt, _ = product(third, gathered, scalars)
    dots, carry, kept = small(
        update_three,
        rhs,
        [spare, (5, rhs, own), spare],
        dealt,
        packed,
        first,
        second,
        third,
        scalars,
    )
    return tuple(small(update_four, rhs, [vector, vector], all_sum(dots), carry, kept))


def solution(mesh):
    placed = (P(None, AXES), P(None, AXES), P(AXES))

    def whole(right_side, points, star_noise):
        return jax.shard_map(
            functools.partial(on_device, right_side.shape[1]),
            mesh=mesh,
            in_specs=placed,
            out_specs=(P(None, AXES), P(None, AXES)),
            check_vma=False,
        )(right_side, points, star_noise)

    return whole
```

```python
import functools
import math

import jax
import jax.numpy as jnp
from jax import lax
from jax.experimental import pallas as pl
from jax.experimental.pallas import tpu as pltpu
from jax.sharding import PartitionSpec as P

QUAD_XX = 1.6
QUAD_XY = 0.5
QUAD_YY = 0.7
INVERSE_SQUARE = 25.0
KERNEL_WEIGHT = 2048.0

LOG2E = math.log2(math.e)
PX = math.sqrt(QUAD_XX * INVERSE_SQUARE)
PY = QUAD_XY * INVERSE_SQUARE / PX
QY = math.sqrt(QUAD_YY * INVERSE_SQUARE - PY * PY)
PX, PY, QY = PX * LOG2E, PY * LOG2E, QY * LOG2E

AXES = ("row", "col")
DEVICES = 256
LANES = 128
SPARE = 8
TILE = 256
VMEM_LIMIT = 24 * 1024 * 1024


def place(index):
    row, col = divmod(index, 16)
    y, z_lo = divmod(row, 4)
    x, rest = divmod(col, 4)
    z_hi, core = divmod(rest, 2)
    return {"x": x, "y": y, "z": z_hi * 4 + z_lo, "core": core}


def number(at):
    row = at["y"] * 4 + at["z"] % 4
    return row * 16 + at["x"] * 4 + (at["z"] // 4) * 2 + at["core"]


def groups_along(*axes):
    groups = {}
    for index in range(DEVICES):
        rest = tuple(v for k, v in place(index).items() if k not in axes)
        groups.setdefault(rest, []).append(index)
    return list(groups.values())


PLANES = groups_along("x", "y")
LINES = groups_along("z")
COLUMNS = groups_along("z", "core")
NEAR = (3, 2, 1)
BLOCKS = (0,) + NEAR + tuple(7 ^ m for m in (0,) + NEAR)


def exchange(value, axis, mask):
    pairs = []
    for index in range(DEVICES):
        at = place(index)
        at[axis] ^= mask
        pairs.append((index, number(at)))
    return lax.ppermute(value, AXES, pairs)


def near_and_far(block):
    near = jnp.concatenate([block] + [exchange(block, "z", m) for m in NEAR], axis=0)
    return near, exchange(near, "z", 7)


def deal(blocks, groups):
    count = len(groups[0])
    rows = blocks.shape[0] // count
    dealt = lax.all_to_all(
        blocks.reshape(count, rows, LANES), AXES, 0, 0, axis_index_groups=groups
    )
    return dealt.reshape(count * rows, LANES)


def all_sum(block):
    for groups in (PLANES, COLUMNS):
        copies = jnp.broadcast_to(block[None], (len(groups[0]),) + block.shape)
        dealt = lax.all_to_all(copies, AXES, 0, 0, axis_index_groups=groups)
        block = jnp.sum(dealt, axis=0)
    return block


def split(vectors):
    high = vectors.astype(jnp.bfloat16)
    low = (vectors - high.astype(jnp.float32)).astype(jnp.bfloat16)
    return high, low


def as_columns(row, rhs):
    return jnp.broadcast_to(row, (LANES, LANES)).T[:rhs, :]


def put_pair(pair_ref, b, block, rhs):
    high, low = split(block)
    pair_ref[:rhs, b * LANES : (b + 1) * LANES] = high
    pair_ref[rhs:, b * LANES : (b + 1) * LANES] = low


def four_terms(pair, kernel, rhs):
    terms = jnp.dot(pair, kernel, preferred_element_type=jnp.float32)
    high, low = terms[:, :TILE], terms[:, TILE:]
    return high[:rhs] + ((high[rhs:] + low[:rhs]) + low[rhs:])


def first_body(rhs, amplitude, has_before, v_ref, rows_ref, *refs):
    before_ref, refs = (refs[0], refs[1:]) if has_before else (None, refs)
    out_ref, kernel_ref, pair_ref, p_ref, q_ref = refs
    step = rhs + SPARE
    tiles, stars, _ = kernel_ref.shape
    for b in range(stars // LANES):
        at = b * step + rhs
        put_pair(pair_ref, b, v_ref[at - rhs : at, :], rhs)
        x, y = v_ref[at : at + 1, :], v_ref[at + 1 : at + 2, :]
        rows = slice(b * LANES, (b + 1) * LANES)
        p_ref[rows, :] = as_columns(PX * x + PY * y, LANES)
        q_ref[rows, :] = as_columns(QY * y, LANES)

    for tile in range(tiles):
        product = jnp.zeros((rhs, TILE), jnp.float32)
        for j in range(0, stars, TILE):
            pieces = []
            for piece in range(TILE // LANES):
                at = (tile * (TILE // LANES) + piece) * SPARE
                x, y = rows_ref[at : at + 1, :], rows_ref[at + 1 : at + 2, :]
                delta_p = p_ref[j : j + TILE, :] - (PX * x + PY * y)
                delta_q = q_ref[j : j + TILE, :] - QY * y
                square = delta_p * delta_p + delta_q * delta_q
                distance = square * lax.rsqrt(jnp.maximum(square, 1e-30))
                pieces.append(split(jnp.exp2(-distance)))
            high = jnp.concatenate([h for h, _ in pieces], axis=1)
            low = jnp.concatenate([l for _, l in pieces], axis=1)
            both = jnp.concatenate([high, low], axis=1)
            kernel_ref[tile, j : j + TILE, :] = both
            product = product + four_terms(pair_ref[:, j : j + TILE], both, rhs)
        for piece in range(TILE // LANES):
            at = (tile * (TILE // LANES) + piece) * rhs
            part = product[:, piece * LANES : (piece + 1) * LANES] * amplitude
            if has_before:
                part = part + before_ref[at : at + rhs, :]
            out_ref[at : at + rhs, :] = part


def next_body(rhs, amplitude, has_last, has_before, v_ref, right_near_ref, right_far_ref, *refs):
    last_ref, scalars_ref, refs = (refs[0], refs[1], refs[2:]) if has_last else (None, None, refs)
    before_ref, refs = (refs[0], refs[1:]) if has_before else (None, refs)
    kernel_refs, out_ref, pair_ref = refs[:2], refs[2], refs[3]
    step = rhs + SPARE
    z_lo = lax.rem(lax.axis_index("row"), 4)
    z_hi = lax.rem(lax.div(lax.axis_index("col"), 2), 2)
    if has_last:
        alpha = as_columns(scalars_ref[0:1, :] / scalars_ref[1:2, :], rhs)
    norm = jnp.zeros((rhs, LANES), jnp.float32)
    curve = jnp.zeros((rhs, LANES), jnp.float32)
    half = len(BLOCKS) // 2
    for b, mask in enumerate(BLOCKS):
        lo, hi = lax.bitwise_xor(z_lo, mask % 4), lax.bitwise_xor(z_hi, mask // 4)
        at = pl.multiple_of((lo * 2 + hi) * rhs, rhs)
        block = v_ref[pl.ds(at, rhs), :]
        put_pair(pair_ref, b, block, rhs)
        right_ref = right_near_ref if b < half else right_far_ref
        residual = right_ref[b % half * step : b % half * step + rhs, :]
        if has_last:
            residual = residual - alpha * last_ref[pl.ds(at, rhs), :]
        norm = norm + residual * residual
        curve = curve + residual * block
    ones = jnp.ones((rhs, LANES), jnp.float32)
    dots = to_rows([dot(norm, ones), dot(curve, ones)], rhs)
    if has_before:
        dots = dots + before_ref[rhs:step, :]

    columns = half * LANES
    for tile in range(kernel_refs[0].shape[0]):
        near, far = (
            four_terms(pair_ref[:, n * columns : (n + 1) * columns], kernel_refs[n][tile], rhs)
            for n in range(2)
        )
        product = near + far
        for piece in range(TILE // LANES):
            at = (tile * (TILE // LANES) + piece) * step
            part = product[:, piece * LANES : (piece + 1) * LANES] * amplitude
            if has_before:
                part = part + before_ref[at : at + rhs, :]
            out_ref[at : at + rhs, :] = part
            out_ref[at + rhs : at + step, :] = dots


def kernel_call(body, outs, scratch, flops, operands):
    whole = pl.BlockSpec(memory_space=pltpu.VMEM)
    return pl.pallas_call(
        body,
        in_specs=[whole] * len(operands),
        out_specs=[whole] * len(outs),
        out_shape=outs,
        scratch_shapes=scratch,
        cost_estimate=pl.CostEstimate(flops=flops, bytes_accessed=0, transcendentals=0),
        compiler_params=pltpu.CompilerParams(vmem_limit_bytes=VMEM_LIMIT),
    )(*operands)


def first_product(part, row_points, before, rhs, amplitude):
    columns = part.shape[0] // (rhs + SPARE) * LANES
    pieces = row_points.shape[0] // SPARE
    outs = [
        jax.ShapeDtypeStruct((pieces * rhs, LANES), jnp.float32),
        jax.ShapeDtypeStruct((pieces * LANES // TILE, columns, 2 * TILE), jnp.bfloat16),
    ]
    scratch = [
        pltpu.VMEM((2 * rhs, columns), jnp.bfloat16),
        pltpu.VMEM((columns, LANES), jnp.float32),
        pltpu.VMEM((columns, LANES), jnp.float32),
    ]
    operands = [part, row_points] + ([] if before is None else [before])
    body = functools.partial(first_body, rhs, amplitude, before is not None)
    return kernel_call(body, outs, scratch, 3 << 30, operands)


def next_product(vectors, rights, last, scalars, before, kernels, rhs, amplitude):
    tiles, columns, _ = kernels[0].shape
    rows = tiles * (TILE // LANES) * (rhs + SPARE)
    outs = [jax.ShapeDtypeStruct((rows, LANES), jnp.float32)]
    scratch = [pltpu.VMEM((2 * rhs, 2 * columns), jnp.bfloat16)]
    operands = [vectors, *rights]
    operands += [] if last is None else [last, scalars]
    operands += [] if before is None else [before]
    operands += kernels
    body = functools.partial(next_body, rhs, amplitude, last is not None, before is not None)
    return kernel_call(body, outs, scratch, 1 << 31, operands)[0]


def dot(a, b):
    return jnp.sum(a * b, axis=1, keepdims=True)


def to_rows(columns, rhs):
    lane = lax.broadcasted_iota(jnp.int32, (rhs, LANES), 1)
    tile = jnp.zeros((rhs, LANES), jnp.float32)
    for i, column in enumerate(columns):
        tile = jnp.where(lane == i, column, tile)
    square = jnp.concatenate([tile, jnp.zeros((LANES - rhs, LANES), jnp.float32)], axis=0)
    return square.T[:SPARE, :]


def pack(rhs, right_ref, points_ref, noise_ref, out_ref, places_ref, spare_ref, semaphores):
    spare_ref[...] = jnp.zeros_like(spare_ref)
    copies = [
        pltpu.make_async_copy(right_ref, out_ref.at[pl.ds(0, rhs), :], semaphores.at[0]),
        pltpu.make_async_copy(points_ref, spare_ref.at[pl.ds(0, 2), :], semaphores.at[1]),
        pltpu.make_async_copy(noise_ref, spare_ref.at[pl.ds(2, 1), :], semaphores.at[2]),
    ]
    for copy in copies:
        copy.start()
    for copy in copies:
        copy.wait()
    spare = spare_ref[...]
    out_ref[rhs:, :] = spare
    for at in range(0, places_ref.shape[0], SPARE):
        places_ref[at : at + SPARE, :] = spare


def packed_inputs(right_side, points, noise):
    rhs, own = right_side.shape
    anywhere, whole = pl.BlockSpec(memory_space=pl.ANY), pl.BlockSpec(memory_space=pltpu.VMEM)
    return pl.pallas_call(
        functools.partial(pack, rhs),
        in_specs=[anywhere] * 3,
        out_specs=[whole] * 2,
        out_shape=[
            jax.ShapeDtypeStruct((rhs + SPARE, own), jnp.float32),
            jax.ShapeDtypeStruct((SPARE * len(PLANES[0]), own), jnp.float32),
        ],
        scratch_shapes=[pltpu.VMEM((SPARE, own), jnp.float32), pltpu.SemaphoreType.DMA((3,))],
        compiler_params=pltpu.CompilerParams(vmem_limit_bytes=60 * 1024 * 1024),
    )(right_side, points, noise)


def summed(dealt_ref, step):
    blocks = [dealt_ref[at : at + step, :] for at in range(0, dealt_ref.shape[0], step)]
    while len(blocks) > 1:
        blocks = [a + b for a, b in zip(blocks[::2], blocks[1::2])]
    return blocks[0]


def right_and_noise(packed_ref, rhs):
    return packed_ref[:rhs, :], packed_ref[rhs + 2 : rhs + 3, :]


def copy_out(copies_ref, vectors):
    rows = vectors.shape[0]
    for at in range(0, copies_ref.shape[0], rows):
        copies_ref[at : at + rows, :] = vectors


def update_one(rhs, dealt_ref, packed_ref, copies_ref):
    right, noise = right_and_noise(packed_ref, rhs)
    copy_out(copies_ref, summed(dealt_ref, rhs) + noise * right)


def update_two(rhs, dealt_ref, packed_ref, first_ref, copies_ref, second_ref, scalars_ref):
    right, noise = right_and_noise(packed_ref, rhs)
    w0 = first_ref[:rhs, :]
    image = summed(dealt_ref, rhs + SPARE)
    dots = image[rhs:, :]
    n0 = image[:rhs, :] + noise * w0
    alpha = as_columns(dots[0:1, :] / dots[1:2, :], rhs)
    copy_out(copies_ref, w0 - alpha * n0)
    second_ref[...] = n0
    scalars_ref[...] = dots


def update_three(rhs, dealt_ref, packed_ref, first_ref, second_ref, third_ref, scalars_ref, dots_ref, carry_ref, kept_ref):
    right, noise = right_and_noise(packed_ref, rhs)
    w0 = first_ref[:rhs, :]
    n0 = second_ref[...]
    w1 = third_ref[:rhs, :]
    image = summed(dealt_ref, rhs + SPARE)
    dots = image[rhs:, :]
    n1 = image[:rhs, :] + noise * w1
    norm0, curve0 = scalars_ref[0:1, :], scalars_ref[1:2, :]
    norm1, curve1 = dots[0:1, :], dots[1:2, :]
    alpha0_row = norm0 / curve0
    beta1_row = norm1 / norm0
    alpha1_row = norm1 / (curve1 - beta1_row * norm1 / alpha0_row)
    alpha0, beta1, alpha1 = (as_columns(row, rhs) for row in (alpha0_row, beta1_row, alpha1_row))
    r1 = right - alpha0 * w0
    s1 = w1 + beta1 * w0
    p1 = r1 + beta1 * right
    z1 = n1 + beta1 * n0
    r2 = r1 - alpha1 * s1
    w2 = w1 - alpha1 * z1
    dots_ref[...] = to_rows([dot(r2, r2), dot(r2, w2)], rhs)
    carry_ref[0] = alpha0 * right + alpha1 * p1
    carry_ref[1] = r2
    carry_ref[2] = p1
    carry_ref[3] = s1
    carry_ref[4] = w2
    kept_ref[...] = jnp.concatenate(
        [norm1, alpha1_row, jnp.zeros((SPARE - 2, LANES), jnp.float32)], axis=0
    )


def update_four(rhs, dots_ref, carry_ref, kept_ref, solution_ref, residual_ref):
    norm2, curve2 = dots_ref[0:1, :], dots_ref[1:2, :]
    norm1, alpha1 = kept_ref[0:1, :], kept_ref[1:2, :]
    beta2_row = norm2 / norm1
    alpha2 = as_columns(norm2 / (curve2 - beta2_row * norm2 / alpha1), rhs)
    beta2 = as_columns(beta2_row, rhs)
    r2 = carry_ref[1]
    solution_ref[...] = carry_ref[0] + alpha2 * (r2 + beta2 * carry_ref[2])
    residual_ref[...] = r2 - alpha2 * (carry_ref[4] + beta2 * carry_ref[3])


def small(body, rhs, shapes, *operands):
    outs = [jax.ShapeDtypeStruct(s, jnp.float32) for s in shapes]
    return pl.pallas_call(
        functools.partial(body, rhs),
        out_shape=outs,
        compiler_params=pltpu.CompilerParams(vmem_limit_bytes=VMEM_LIMIT),
    )(*operands)


def on_device(total_stars, right_side, points, star_noise):
    rhs, own = right_side.shape
    amplitude = KERNEL_WEIGHT / total_stars
    vector, spare, copies = (rhs, own), (SPARE, own), (rhs * len(BLOCKS), own)

    packed, places = packed_inputs(right_side, points, star_noise[None, :])
    row_points = deal(places, PLANES)
    rights, kernels, pieces = [], [], None
    near, far = near_and_far(packed)
    for n, half in enumerate((near, far)):
        if n == 1:
            half, pieces = lax.optimization_barrier((half, pieces))
        for part in (half, exchange(half, "core", 1)):
            pieces, kernel = first_product(part, row_points, pieces, rhs, amplitude)
            kernels.append(kernel)
            rights.append(part)
    (first,) = small(update_one, rhs, [copies], deal(pieces, PLANES), packed)

    def product(vectors, lasts, scalars):
        mine = deal(vectors, LINES)
        other = exchange(mine, "core", 1)
        pieces = None
        for n, part in enumerate((mine, other)):
            pieces = next_product(
                part, rights[n::2], lasts[n], scalars, pieces, kernels[n::2], rhs, amplitude
            )
        return deal(pieces, PLANES), (mine, other)

    dealt, gathered = product(first, (None, None), None)
    third, second, scalars = small(
        update_two, rhs, [copies, vector, spare], dealt, packed, first
    )
    dealt, _ = product(third, gathered, scalars)
    dots, carry, kept = small(
        update_three,
        rhs,
        [spare, (5, rhs, own), spare],
        dealt,
        packed,
        first,
        second,
        third,
        scalars,
    )
    return tuple(small(update_four, rhs, [vector, vector], all_sum(dots), carry, kept))


def solution(mesh):
    placed = (P(None, AXES), P(None, AXES), P(AXES))

    def whole(right_side, points, star_noise):
        return jax.shard_map(
            functools.partial(on_device, right_side.shape[1]),
            mesh=mesh,
            in_specs=placed,
            out_specs=(P(None, AXES), P(None, AXES)),
            check_vma=False,
        )(right_side, points, star_noise)

    return whole
```

```python
import functools
import math

import jax
import jax.numpy as jnp
from jax import lax
from jax.experimental import pallas as pl
from jax.experimental.pallas import tpu as pltpu
from jax.sharding import PartitionSpec as P

QUAD_XX = 1.6
QUAD_XY = 0.5
QUAD_YY = 0.7
INVERSE_SQUARE = 25.0
KERNEL_WEIGHT = 2048.0

LOG2E = math.log2(math.e)
PX = math.sqrt(QUAD_XX * INVERSE_SQUARE)
PY = QUAD_XY * INVERSE_SQUARE / PX
QY = math.sqrt(QUAD_YY * INVERSE_SQUARE - PY * PY)
PX, PY, QY = PX * LOG2E, PY * LOG2E, QY * LOG2E

AXES = ("row", "col")
DEVICES = 256
LANES = 128
SPARE = 8
TILE = 256
VMEM_LIMIT = 24 * 1024 * 1024


def place(index):
    row, col = divmod(index, 16)
    y, z_lo = divmod(row, 4)
    x, rest = divmod(col, 4)
    z_hi, core = divmod(rest, 2)
    return {"x": x, "y": y, "z": z_hi * 4 + z_lo, "core": core}


def number(at):
    row = at["y"] * 4 + at["z"] % 4
    return row * 16 + at["x"] * 4 + (at["z"] // 4) * 2 + at["core"]


def groups_along(*axes):
    groups = {}
    for index in range(DEVICES):
        rest = tuple(v for k, v in place(index).items() if k not in axes)
        groups.setdefault(rest, []).append(index)
    return list(groups.values())


PLANES = groups_along("x", "y")
LINES = groups_along("z")
COLUMNS = groups_along("z", "core")
NEAR, FAR = (2, 5, 7), 1
BLOCKS = (0,) + NEAR + tuple(FAR ^ m for m in (0,) + NEAR)


def exchange(value, axis, mask):
    pairs = []
    for index in range(DEVICES):
        at = place(index)
        at[axis] ^= mask
        pairs.append((index, number(at)))
    return lax.ppermute(value, AXES, pairs)


def near_and_far(block):
    near = jnp.concatenate([block] + [exchange(block, "z", m) for m in NEAR], axis=0)
    return near, exchange(near, "z", FAR)


def deal(blocks, groups):
    count = len(groups[0])
    rows = blocks.shape[0] // count
    dealt = lax.all_to_all(
        blocks.reshape(count, rows, LANES), AXES, 0, 0, axis_index_groups=groups
    )
    return dealt.reshape(count * rows, LANES)


def all_sum(block):
    for groups in (PLANES, COLUMNS):
        copies = jnp.broadcast_to(block[None], (len(groups[0]),) + block.shape)
        dealt = lax.all_to_all(copies, AXES, 0, 0, axis_index_groups=groups)
        block = jnp.sum(dealt, axis=0)
    return block


def split(vectors):
    high = vectors.astype(jnp.bfloat16)
    low = (vectors - high.astype(jnp.float32)).astype(jnp.bfloat16)
    return high, low


def as_columns(row, rhs):
    return jnp.broadcast_to(row, (LANES, LANES)).T[:rhs, :]


def put_pair(pair_ref, b, block, rhs):
    high, low = split(block)
    pair_ref[:rhs, b * LANES : (b + 1) * LANES] = high
    pair_ref[rhs:, b * LANES : (b + 1) * LANES] = low


def four_terms(pair, kernel, rhs):
    terms = jnp.dot(pair, kernel, preferred_element_type=jnp.float32)
    high, low = terms[:, :TILE], terms[:, TILE:]
    return high[:rhs] + ((high[rhs:] + low[:rhs]) + low[rhs:])


def first_body(rhs, amplitude, has_before, v_ref, rows_ref, *refs):
    before_ref, refs = (refs[0], refs[1:]) if has_before else (None, refs)
    out_ref, kernel_ref, pair_ref, p_ref, q_ref = refs
    step = rhs + SPARE
    tiles, stars, _ = kernel_ref.shape
    for b in range(stars // LANES):
        at = b * step + rhs
        put_pair(pair_ref, b, v_ref[at - rhs : at, :], rhs)
        x, y = v_ref[at : at + 1, :], v_ref[at + 1 : at + 2, :]
        rows = slice(b * LANES, (b + 1) * LANES)
        p_ref[rows, :] = as_columns(PX * x + PY * y, LANES)
        q_ref[rows, :] = as_columns(QY * y, LANES)

    for tile in range(tiles):
        product = jnp.zeros((rhs, TILE), jnp.float32)
        for j in range(0, stars, TILE):
            pieces = []
            for piece in range(TILE // LANES):
                at = (tile * (TILE // LANES) + piece) * SPARE
                x, y = rows_ref[at : at + 1, :], rows_ref[at + 1 : at + 2, :]
                delta_p = p_ref[j : j + TILE, :] - (PX * x + PY * y)
                delta_q = q_ref[j : j + TILE, :] - QY * y
                square = delta_p * delta_p + delta_q * delta_q
                distance = square * lax.rsqrt(jnp.maximum(square, 1e-30))
                pieces.append(split(jnp.exp2(-distance)))
            high = jnp.concatenate([h for h, _ in pieces], axis=1)
            low = jnp.concatenate([l for _, l in pieces], axis=1)
            both = jnp.concatenate([high, low], axis=1)
            kernel_ref[tile, j : j + TILE, :] = both
            product = product + four_terms(pair_ref[:, j : j + TILE], both, rhs)
        for piece in range(TILE // LANES):
            at = (tile * (TILE // LANES) + piece) * rhs
            part = product[:, piece * LANES : (piece + 1) * LANES] * amplitude
            if has_before:
                part = part + before_ref[at : at + rhs, :]
            out_ref[at : at + rhs, :] = part


def next_body(rhs, amplitude, has_last, has_before, v_ref, right_near_ref, right_far_ref, *refs):
    last_ref, scalars_ref, refs = (refs[0], refs[1], refs[2:]) if has_last else (None, None, refs)
    before_ref, refs = (refs[0], refs[1:]) if has_before else (None, refs)
    kernel_refs, out_ref, pair_ref = refs[:2], refs[2], refs[3]
    step = rhs + SPARE
    z_lo = lax.rem(lax.axis_index("row"), 4)
    z_hi = lax.rem(lax.div(lax.axis_index("col"), 2), 2)
    if has_last:
        alpha = as_columns(scalars_ref[0:1, :] / scalars_ref[1:2, :], rhs)
    norm = jnp.zeros((rhs, LANES), jnp.float32)
    curve = jnp.zeros((rhs, LANES), jnp.float32)
    half = len(BLOCKS) // 2
    for b, mask in enumerate(BLOCKS):
        lo, hi = lax.bitwise_xor(z_lo, mask % 4), lax.bitwise_xor(z_hi, mask // 4)
        at = pl.multiple_of((lo * 2 + hi) * rhs, rhs)
        block = v_ref[pl.ds(at, rhs), :]
        put_pair(pair_ref, b, block, rhs)
        right_ref = right_near_ref if b < half else right_far_ref
        residual = right_ref[b % half * step : b % half * step + rhs, :]
        if has_last:
            residual = residual - alpha * last_ref[pl.ds(at, rhs), :]
        norm = norm + residual * residual
        curve = curve + residual * block
    ones = jnp.ones((rhs, LANES), jnp.float32)
    dots = to_rows([dot(norm, ones), dot(curve, ones)], rhs)
    if has_before:
        dots = dots + before_ref[rhs:step, :]

    columns = half * LANES
    for tile in range(kernel_refs[0].shape[0]):
        near, far = (
            four_terms(pair_ref[:, n * columns : (n + 1) * columns], kernel_refs[n][tile], rhs)
            for n in range(2)
        )
        product = near + far
        for piece in range(TILE // LANES):
            at = (tile * (TILE // LANES) + piece) * step
            part = product[:, piece * LANES : (piece + 1) * LANES] * amplitude
            if has_before:
                part = part + before_ref[at : at + rhs, :]
            out_ref[at : at + rhs, :] = part
            out_ref[at + rhs : at + step, :] = dots


def kernel_call(body, outs, scratch, flops, operands):
    whole = pl.BlockSpec(memory_space=pltpu.VMEM)
    return pl.pallas_call(
        body,
        in_specs=[whole] * len(operands),
        out_specs=[whole] * len(outs),
        out_shape=outs,
        scratch_shapes=scratch,
        cost_estimate=pl.CostEstimate(flops=flops, bytes_accessed=0, transcendentals=0),
        compiler_params=pltpu.CompilerParams(vmem_limit_bytes=VMEM_LIMIT),
    )(*operands)


def first_product(part, row_points, before, rhs, amplitude):
    columns = part.shape[0] // (rhs + SPARE) * LANES
    pieces = row_points.shape[0] // SPARE
    outs = [
        jax.ShapeDtypeStruct((pieces * rhs, LANES), jnp.float32),
        jax.ShapeDtypeStruct((pieces * LANES // TILE, columns, 2 * TILE), jnp.bfloat16),
    ]
    scratch = [
        pltpu.VMEM((2 * rhs, columns), jnp.bfloat16),
        pltpu.VMEM((columns, LANES), jnp.float32),
        pltpu.VMEM((columns, LANES), jnp.float32),
    ]
    operands = [part, row_points] + ([] if before is None else [before])
    body = functools.partial(first_body, rhs, amplitude, before is not None)
    return kernel_call(body, outs, scratch, 3 << 30, operands)


def next_product(vectors, rights, last, scalars, before, kernels, rhs, amplitude):
    tiles, columns, _ = kernels[0].shape
    rows = tiles * (TILE // LANES) * (rhs + SPARE)
    outs = [jax.ShapeDtypeStruct((rows, LANES), jnp.float32)]
    scratch = [pltpu.VMEM((2 * rhs, 2 * columns), jnp.bfloat16)]
    operands = [vectors, *rights]
    operands += [] if last is None else [last, scalars]
    operands += [] if before is None else [before]
    operands += kernels
    body = functools.partial(next_body, rhs, amplitude, last is not None, before is not None)
    return kernel_call(body, outs, scratch, 1 << 31, operands)[0]


def dot(a, b):
    return jnp.sum(a * b, axis=1, keepdims=True)


def to_rows(columns, rhs):
    lane = lax.broadcasted_iota(jnp.int32, (rhs, LANES), 1)
    tile = jnp.zeros((rhs, LANES), jnp.float32)
    for i, column in enumerate(columns):
        tile = jnp.where(lane == i, column, tile)
    square = jnp.concatenate([tile, jnp.zeros((LANES - rhs, LANES), jnp.float32)], axis=0)
    return square.T[:SPARE, :]


def pack(rhs, right_ref, points_ref, noise_ref, out_ref, places_ref, spare_ref, semaphores):
    spare_ref[...] = jnp.zeros_like(spare_ref)
    copies = [
        pltpu.make_async_copy(right_ref, out_ref.at[pl.ds(0, rhs), :], semaphores.at[0]),
        pltpu.make_async_copy(points_ref, spare_ref.at[pl.ds(0, 2), :], semaphores.at[1]),
        pltpu.make_async_copy(noise_ref, spare_ref.at[pl.ds(2, 1), :], semaphores.at[2]),
    ]
    for copy in copies:
        copy.start()
    for copy in copies:
        copy.wait()
    spare = spare_ref[...]
    out_ref[rhs:, :] = spare
    for at in range(0, places_ref.shape[0], SPARE):
        places_ref[at : at + SPARE, :] = spare


def packed_inputs(right_side, points, noise):
    rhs, own = right_side.shape
    anywhere, whole = pl.BlockSpec(memory_space=pl.ANY), pl.BlockSpec(memory_space=pltpu.VMEM)
    return pl.pallas_call(
        functools.partial(pack, rhs),
        in_specs=[anywhere] * 3,
        out_specs=[whole] * 2,
        out_shape=[
            jax.ShapeDtypeStruct((rhs + SPARE, own), jnp.float32),
            jax.ShapeDtypeStruct((SPARE * len(PLANES[0]), own), jnp.float32),
        ],
        scratch_shapes=[pltpu.VMEM((SPARE, own), jnp.float32), pltpu.SemaphoreType.DMA((3,))],
        compiler_params=pltpu.CompilerParams(vmem_limit_bytes=60 * 1024 * 1024),
    )(right_side, points, noise)


def summed(dealt_ref, step):
    blocks = [dealt_ref[at : at + step, :] for at in range(0, dealt_ref.shape[0], step)]
    while len(blocks) > 1:
        blocks = [a + b for a, b in zip(blocks[::2], blocks[1::2])]
    return blocks[0]


def right_and_noise(packed_ref, rhs):
    return packed_ref[:rhs, :], packed_ref[rhs + 2 : rhs + 3, :]


def copy_out(copies_ref, vectors):
    rows = vectors.shape[0]
    for at in range(0, copies_ref.shape[0], rows):
        copies_ref[at : at + rows, :] = vectors


def update_one(rhs, dealt_ref, packed_ref, copies_ref):
    right, noise = right_and_noise(packed_ref, rhs)
    copy_out(copies_ref, summed(dealt_ref, rhs) + noise * right)


def update_two(rhs, dealt_ref, packed_ref, first_ref, copies_ref, second_ref, scalars_ref):
    right, noise = right_and_noise(packed_ref, rhs)
    w0 = first_ref[:rhs, :]
    image = summed(dealt_ref, rhs + SPARE)
    dots = image[rhs:, :]
    n0 = image[:rhs, :] + noise * w0
    alpha = as_columns(dots[0:1, :] / dots[1:2, :], rhs)
    copy_out(copies_ref, w0 - alpha * n0)
    second_ref[...] = n0
    scalars_ref[...] = dots


def update_three(rhs, dealt_ref, packed_ref, first_ref, second_ref, third_ref, scalars_ref, dots_ref, carry_ref, kept_ref):
    right, noise = right_and_noise(packed_ref, rhs)
    w0 = first_ref[:rhs, :]
    n0 = second_ref[...]
    w1 = third_ref[:rhs, :]
    image = summed(dealt_ref, rhs + SPARE)
    dots = image[rhs:, :]
    n1 = image[:rhs, :] + noise * w1
    norm0, curve0 = scalars_ref[0:1, :], scalars_ref[1:2, :]
    norm1, curve1 = dots[0:1, :], dots[1:2, :]
    alpha0_row = norm0 / curve0
    beta1_row = norm1 / norm0
    alpha1_row = norm1 / (curve1 - beta1_row * norm1 / alpha0_row)
    alpha0, beta1, alpha1 = (as_columns(row, rhs) for row in (alpha0_row, beta1_row, alpha1_row))
    r1 = right - alpha0 * w0
    s1 = w1 + beta1 * w0
    p1 = r1 + beta1 * right
    z1 = n1 + beta1 * n0
    r2 = r1 - alpha1 * s1
    w2 = w1 - alpha1 * z1
    dots_ref[...] = to_rows([dot(r2, r2), dot(r2, w2)], rhs)
    carry_ref[0] = alpha0 * right + alpha1 * p1
    carry_ref[1] = r2
    carry_ref[2] = p1
    carry_ref[3] = s1
    carry_ref[4] = w2
    kept_ref[...] = jnp.concatenate(
        [norm1, alpha1_row, jnp.zeros((SPARE - 2, LANES), jnp.float32)], axis=0
    )


def update_four(rhs, dots_ref, carry_ref, kept_ref, solution_ref, residual_ref):
    norm2, curve2 = dots_ref[0:1, :], dots_ref[1:2, :]
    norm1, alpha1 = kept_ref[0:1, :], kept_ref[1:2, :]
    beta2_row = norm2 / norm1
    alpha2 = as_columns(norm2 / (curve2 - beta2_row * norm2 / alpha1), rhs)
    beta2 = as_columns(beta2_row, rhs)
    r2 = carry_ref[1]
    solution_ref[...] = carry_ref[0] + alpha2 * (r2 + beta2 * carry_ref[2])
    residual_ref[...] = r2 - alpha2 * (carry_ref[4] + beta2 * carry_ref[3])


def small(body, rhs, shapes, *operands):
    outs = [jax.ShapeDtypeStruct(s, jnp.float32) for s in shapes]
    return pl.pallas_call(
        functools.partial(body, rhs),
        out_shape=outs,
        compiler_params=pltpu.CompilerParams(vmem_limit_bytes=VMEM_LIMIT),
    )(*operands)


def on_device(total_stars, right_side, points, star_noise):
    rhs, own = right_side.shape
    amplitude = KERNEL_WEIGHT / total_stars
    vector, spare, copies = (rhs, own), (SPARE, own), (rhs * len(BLOCKS), own)

    packed, places = packed_inputs(right_side, points, star_noise[None, :])
    row_points = deal(places, PLANES)
    rights, kernels, pieces = [], [], None
    near, far = near_and_far(packed)
    for n, half in enumerate((near, far)):
        if n == 1:
            half, pieces = lax.optimization_barrier((half, pieces))
        for part in (half, exchange(half, "core", 1)):
            pieces, kernel = first_product(part, row_points, pieces, rhs, amplitude)
            kernels.append(kernel)
            rights.append(part)
    (first,) = small(update_one, rhs, [copies], deal(pieces, PLANES), packed)

    def product(vectors, lasts, scalars):
        mine = deal(vectors, LINES)
        other = exchange(mine, "core", 1)
        pieces = None
        for n, part in enumerate((mine, other)):
            pieces = next_product(
                part, rights[n::2], lasts[n], scalars, pieces, kernels[n::2], rhs, amplitude
            )
        return deal(pieces, PLANES), (mine, other)

    dealt, gathered = product(first, (None, None), None)
    third, second, scalars = small(
        update_two, rhs, [copies, vector, spare], dealt, packed, first
    )
    dealt, _ = product(third, gathered, scalars)
    dots, carry, kept = small(
        update_three,
        rhs,
        [spare, (5, rhs, own), spare],
        dealt,
        packed,
        first,
        second,
        third,
        scalars,
    )
    return tuple(small(update_four, rhs, [vector, vector], all_sum(dots), carry, kept))


def solution(mesh):
    placed = (P(None, AXES), P(None, AXES), P(AXES))

    def whole(right_side, points, star_noise):
        return jax.shard_map(
            functools.partial(on_device, right_side.shape[1]),
            mesh=mesh,
            in_specs=placed,
            out_specs=(P(None, AXES), P(None, AXES)),
            check_vma=False,
        )(right_side, points, star_noise)

    return whole
```

```python
import functools
import math

import jax
import jax.numpy as jnp
from jax import lax
from jax.experimental import pallas as pl
from jax.experimental.pallas import tpu as pltpu
from jax.sharding import PartitionSpec as P

QUAD_XX = 1.6
QUAD_XY = 0.5
QUAD_YY = 0.7
INVERSE_SQUARE = 25.0
KERNEL_WEIGHT = 2048.0

LOG2E = math.log2(math.e)
PX = math.sqrt(QUAD_XX * INVERSE_SQUARE)
PY = QUAD_XY * INVERSE_SQUARE / PX
QY = math.sqrt(QUAD_YY * INVERSE_SQUARE - PY * PY)
PX, PY, QY = PX * LOG2E, PY * LOG2E, QY * LOG2E

AXES = ("row", "col")
DEVICES = 256
LANES = 128
SPARE = 8
TILE = 256
VMEM_LIMIT = 24 * 1024 * 1024


def place(index):
    row, col = divmod(index, 16)
    y, z_lo = divmod(row, 4)
    x, rest = divmod(col, 4)
    z_hi, core = divmod(rest, 2)
    return {"x": x, "y": y, "z": z_hi * 4 + z_lo, "core": core}


def number(at):
    row = at["y"] * 4 + at["z"] % 4
    return row * 16 + at["x"] * 4 + (at["z"] // 4) * 2 + at["core"]


def bit_reversed(value, bits):
    return sum(((value >> b) & 1) << (bits - 1 - b) for b in range(bits))


def groups_along(*axes, key=None):
    groups = {}
    for index in range(DEVICES):
        rest = tuple(v for k, v in place(index).items() if k not in axes)
        groups.setdefault(rest, []).append(index)
    return [sorted(g, key=None if key is None else lambda i: key(place(i))) for g in groups.values()]


PLANES = groups_along("x", "y")
LINES = groups_along("z", key=lambda at: bit_reversed(at["z"], 3))
NEAR, FAR = (7, 2, 5), 1
BLOCKS = (0,) + NEAR + tuple(FAR ^ m for m in (0,) + NEAR)


def exchange(value, axis, mask):
    pairs = []
    for index in range(DEVICES):
        at = place(index)
        at[axis] ^= mask
        pairs.append((index, number(at)))
    return lax.ppermute(value, AXES, pairs)


def near_and_far(block):
    near = jnp.concatenate([block] + [exchange(block, "z", m) for m in NEAR], axis=0)
    return near, exchange(near, "z", FAR)


def deal(blocks, groups):
    count = len(groups[0])
    rows = blocks.shape[0] // count
    dealt = lax.all_to_all(
        blocks.reshape(count, rows, LANES), AXES, 0, 0, axis_index_groups=groups
    )
    return dealt.reshape(count * rows, LANES)


def all_sum(block):
    block = block + exchange(block, "core", 1)
    for groups in (PLANES, LINES):
        copies = jnp.broadcast_to(block[None], (len(groups[0]),) + block.shape)
        dealt = lax.all_to_all(copies, AXES, 0, 0, axis_index_groups=groups)
        block = jnp.sum(dealt, axis=0)
    return block


def split(vectors):
    high = vectors.astype(jnp.bfloat16)
    low = (vectors - high.astype(jnp.float32)).astype(jnp.bfloat16)
    return high, low


def as_columns(row, rhs):
    return jnp.broadcast_to(row, (LANES, LANES)).T[:rhs, :]


def put_pair(pair_ref, b, block, rhs):
    high, low = split(block)
    pair_ref[:rhs, b * LANES : (b + 1) * LANES] = high
    pair_ref[rhs:, b * LANES : (b + 1) * LANES] = low


def four_terms(pair, kernel, rhs):
    terms = jnp.dot(pair, kernel, preferred_element_type=jnp.float32)
    high, low = terms[:, :TILE], terms[:, TILE:]
    return high[:rhs] + ((high[rhs:] + low[:rhs]) + low[rhs:])


def first_body(rhs, amplitude, has_before, v_ref, rows_ref, *refs):
    before_ref, refs = (refs[0], refs[1:]) if has_before else (None, refs)
    out_ref, kernel_ref, pair_ref, p_ref, q_ref = refs
    step = rhs + SPARE
    tiles, stars, _ = kernel_ref.shape
    for b in range(stars // LANES):
        at = b * step + rhs
        put_pair(pair_ref, b, v_ref[at - rhs : at, :], rhs)
        x, y = v_ref[at : at + 1, :], v_ref[at + 1 : at + 2, :]
        rows = slice(b * LANES, (b + 1) * LANES)
        p_ref[rows, :] = as_columns(PX * x + PY * y, LANES)
        q_ref[rows, :] = as_columns(QY * y, LANES)

    for tile in range(tiles):
        product = jnp.zeros((rhs, TILE), jnp.float32)
        for j in range(0, stars, TILE):
            pieces = []
            for piece in range(TILE // LANES):
                at = (tile * (TILE // LANES) + piece) * SPARE
                x, y = rows_ref[at : at + 1, :], rows_ref[at + 1 : at + 2, :]
                delta_p = p_ref[j : j + TILE, :] - (PX * x + PY * y)
                delta_q = q_ref[j : j + TILE, :] - QY * y
                square = delta_p * delta_p + delta_q * delta_q
                distance = square * lax.rsqrt(jnp.maximum(square, 1e-30))
                pieces.append(split(jnp.exp2(-distance)))
            high = jnp.concatenate([h for h, _ in pieces], axis=1)
            low = jnp.concatenate([l for _, l in pieces], axis=1)
            both = jnp.concatenate([high, low], axis=1)
            kernel_ref[tile, j : j + TILE, :] = both
            product = product + four_terms(pair_ref[:, j : j + TILE], both, rhs)
        for piece in range(TILE // LANES):
            at = (tile * (TILE // LANES) + piece) * rhs
            part = product[:, piece * LANES : (piece + 1) * LANES] * amplitude
            if has_before:
                part = part + before_ref[at : at + rhs, :]
            out_ref[at : at + rhs, :] = part


def next_body(rhs, amplitude, has_last, has_before, v_ref, right_near_ref, right_far_ref, *refs):
    last_ref, scalars_ref, refs = (refs[0], refs[1], refs[2:]) if has_last else (None, None, refs)
    before_ref, refs = (refs[0], refs[1:]) if has_before else (None, refs)
    kernel_refs, out_ref, pair_ref = refs[:2], refs[2], refs[3]
    step = rhs + SPARE
    z_lo = lax.rem(lax.axis_index("row"), 4)
    z_hi = lax.rem(lax.div(lax.axis_index("col"), 2), 2)
    if has_last:
        alpha = as_columns(scalars_ref[0:1, :] / scalars_ref[1:2, :], rhs)
    norm = jnp.zeros((rhs, LANES), jnp.float32)
    curve = jnp.zeros((rhs, LANES), jnp.float32)
    half = len(BLOCKS) // 2
    for b, mask in enumerate(BLOCKS):
        lo, hi = lax.bitwise_xor(z_lo, mask % 4), lax.bitwise_xor(z_hi, mask // 4)
        place_in_line = lax.rem(lo, 2) * 4 + lax.div(lo, 2) * 2 + hi
        at = pl.multiple_of(place_in_line * rhs, rhs)
        block = v_ref[pl.ds(at, rhs), :]
        put_pair(pair_ref, b, block, rhs)
        right_ref = right_near_ref if b < half else right_far_ref
        residual = right_ref[b % half * step : b % half * step + rhs, :]
        if has_last:
            residual = residual - alpha * last_ref[pl.ds(at, rhs), :]
        norm = norm + residual * residual
        curve = curve + residual * block
    ones = jnp.ones((rhs, LANES), jnp.float32)
    dots = to_rows([dot(norm, ones), dot(curve, ones)], rhs)
    if has_before:
        dots = dots + before_ref[rhs:step, :]

    columns = half * LANES
    for tile in range(kernel_refs[0].shape[0]):
        near, far = (
            four_terms(pair_ref[:, n * columns : (n + 1) * columns], kernel_refs[n][tile], rhs)
            for n in range(2)
        )
        product = near + far
        for piece in range(TILE // LANES):
            at = (tile * (TILE // LANES) + piece) * step
            part = product[:, piece * LANES : (piece + 1) * LANES] * amplitude
            if has_before:
                part = part + before_ref[at : at + rhs, :]
            out_ref[at : at + rhs, :] = part
            out_ref[at + rhs : at + step, :] = dots


def kernel_call(body, outs, scratch, flops, operands):
    whole = pl.BlockSpec(memory_space=pltpu.VMEM)
    return pl.pallas_call(
        body,
        in_specs=[whole] * len(operands),
        out_specs=[whole] * len(outs),
        out_shape=outs,
        scratch_shapes=scratch,
        cost_estimate=pl.CostEstimate(flops=flops, bytes_accessed=0, transcendentals=0),
        compiler_params=pltpu.CompilerParams(vmem_limit_bytes=VMEM_LIMIT),
    )(*operands)


def first_product(part, row_points, before, rhs, amplitude):
    columns = part.shape[0] // (rhs + SPARE) * LANES
    pieces = row_points.shape[0] // SPARE
    outs = [
        jax.ShapeDtypeStruct((pieces * rhs, LANES), jnp.float32),
        jax.ShapeDtypeStruct((pieces * LANES // TILE, columns, 2 * TILE), jnp.bfloat16),
    ]
    scratch = [
        pltpu.VMEM((2 * rhs, columns), jnp.bfloat16),
        pltpu.VMEM((columns, LANES), jnp.float32),
        pltpu.VMEM((columns, LANES), jnp.float32),
    ]
    operands = [part, row_points] + ([] if before is None else [before])
    body = functools.partial(first_body, rhs, amplitude, before is not None)
    return kernel_call(body, outs, scratch, 3 << 30, operands)


def next_product(vectors, rights, last, scalars, before, kernels, rhs, amplitude):
    tiles, columns, _ = kernels[0].shape
    rows = tiles * (TILE // LANES) * (rhs + SPARE)
    outs = [jax.ShapeDtypeStruct((rows, LANES), jnp.float32)]
    scratch = [pltpu.VMEM((2 * rhs, 2 * columns), jnp.bfloat16)]
    operands = [vectors, *rights]
    operands += [] if last is None else [last, scalars]
    operands += [] if before is None else [before]
    operands += kernels
    body = functools.partial(next_body, rhs, amplitude, last is not None, before is not None)
    return kernel_call(body, outs, scratch, 1 << 31, operands)[0]


def dot(a, b):
    return jnp.sum(a * b, axis=1, keepdims=True)


def to_rows(columns, rhs):
    lane = lax.broadcasted_iota(jnp.int32, (rhs, LANES), 1)
    tile = jnp.zeros((rhs, LANES), jnp.float32)
    for i, column in enumerate(columns):
        tile = jnp.where(lane == i, column, tile)
    square = jnp.concatenate([tile, jnp.zeros((LANES - rhs, LANES), jnp.float32)], axis=0)
    return square.T[:SPARE, :]


def pack(rhs, right_ref, points_ref, noise_ref, out_ref, places_ref, spare_ref, semaphores):
    spare_ref[...] = jnp.zeros_like(spare_ref)
    copies = [
        pltpu.make_async_copy(right_ref, out_ref.at[pl.ds(0, rhs), :], semaphores.at[0]),
        pltpu.make_async_copy(points_ref, spare_ref.at[pl.ds(0, 2), :], semaphores.at[1]),
        pltpu.make_async_copy(noise_ref, spare_ref.at[pl.ds(2, 1), :], semaphores.at[2]),
    ]
    for copy in copies:
        copy.start()
    for copy in copies:
        copy.wait()
    spare = spare_ref[...]
    out_ref[rhs:, :] = spare
    for at in range(0, places_ref.shape[0], SPARE):
        places_ref[at : at + SPARE, :] = spare


def packed_inputs(right_side, points, noise):
    rhs, own = right_side.shape
    anywhere, whole = pl.BlockSpec(memory_space=pl.ANY), pl.BlockSpec(memory_space=pltpu.VMEM)
    return pl.pallas_call(
        functools.partial(pack, rhs),
        in_specs=[anywhere] * 3,
        out_specs=[whole] * 2,
        out_shape=[
            jax.ShapeDtypeStruct((rhs + SPARE, own), jnp.float32),
            jax.ShapeDtypeStruct((SPARE * len(PLANES[0]), own), jnp.float32),
        ],
        scratch_shapes=[pltpu.VMEM((SPARE, own), jnp.float32), pltpu.SemaphoreType.DMA((3,))],
        compiler_params=pltpu.CompilerParams(vmem_limit_bytes=60 * 1024 * 1024),
    )(right_side, points, noise)


def summed(dealt_ref, step):
    blocks = [dealt_ref[at : at + step, :] for at in range(0, dealt_ref.shape[0], step)]
    while len(blocks) > 1:
        blocks = [a + b for a, b in zip(blocks[::2], blocks[1::2])]
    return blocks[0]


def right_and_noise(packed_ref, rhs):
    return packed_ref[:rhs, :], packed_ref[rhs + 2 : rhs + 3, :]


def copy_out(copies_ref, vectors):
    rows = vectors.shape[0]
    for at in range(0, copies_ref.shape[0], rows):
        copies_ref[at : at + rows, :] = vectors


def update_one(rhs, dealt_ref, packed_ref, copies_ref):
    right, noise = right_and_noise(packed_ref, rhs)
    copy_out(copies_ref, summed(dealt_ref, rhs) + noise * right)


def update_two(rhs, dealt_ref, packed_ref, first_ref, copies_ref, second_ref, scalars_ref):
    right, noise = right_and_noise(packed_ref, rhs)
    w0 = first_ref[:rhs, :]
    image = summed(dealt_ref, rhs + SPARE)
    dots = image[rhs:, :]
    n0 = image[:rhs, :] + noise * w0
    alpha = as_columns(dots[0:1, :] / dots[1:2, :], rhs)
    copy_out(copies_ref, w0 - alpha * n0)
    second_ref[...] = n0
    scalars_ref[...] = dots


def update_three(rhs, dealt_ref, packed_ref, first_ref, second_ref, third_ref, scalars_ref, dots_ref, carry_ref, kept_ref):
    right, noise = right_and_noise(packed_ref, rhs)
    w0 = first_ref[:rhs, :]
    n0 = second_ref[...]
    w1 = third_ref[:rhs, :]
    image = summed(dealt_ref, rhs + SPARE)
    dots = image[rhs:, :]
    n1 = image[:rhs, :] + noise * w1
    norm0, curve0 = scalars_ref[0:1, :], scalars_ref[1:2, :]
    norm1, curve1 = dots[0:1, :], dots[1:2, :]
    alpha0_row = norm0 / curve0
    beta1_row = norm1 / norm0
    alpha1_row = norm1 / (curve1 - beta1_row * norm1 / alpha0_row)
    alpha0, beta1, alpha1 = (as_columns(row, rhs) for row in (alpha0_row, beta1_row, alpha1_row))
    r1 = right - alpha0 * w0
    s1 = w1 + beta1 * w0
    p1 = r1 + beta1 * right
    z1 = n1 + beta1 * n0
    r2 = r1 - alpha1 * s1
    w2 = w1 - alpha1 * z1
    dots_ref[...] = to_rows([dot(r2, r2), dot(r2, w2)], rhs)
    carry_ref[0] = alpha0 * right + alpha1 * p1
    carry_ref[1] = r2
    carry_ref[2] = p1
    carry_ref[3] = s1
    carry_ref[4] = w2
    kept_ref[...] = jnp.concatenate(
        [norm1, alpha1_row, jnp.zeros((SPARE - 2, LANES), jnp.float32)], axis=0
    )


def update_four(rhs, dots_ref, carry_ref, kept_ref, solution_ref, residual_ref):
    norm2, curve2 = dots_ref[0:1, :], dots_ref[1:2, :]
    norm1, alpha1 = kept_ref[0:1, :], kept_ref[1:2, :]
    beta2_row = norm2 / norm1
    alpha2 = as_columns(norm2 / (curve2 - beta2_row * norm2 / alpha1), rhs)
    beta2 = as_columns(beta2_row, rhs)
    r2 = carry_ref[1]
    solution_ref[...] = carry_ref[0] + alpha2 * (r2 + beta2 * carry_ref[2])
    residual_ref[...] = r2 - alpha2 * (carry_ref[4] + beta2 * carry_ref[3])


def small(body, rhs, shapes, *operands):
    outs = [jax.ShapeDtypeStruct(s, jnp.float32) for s in shapes]
    return pl.pallas_call(
        functools.partial(body, rhs),
        out_shape=outs,
        compiler_params=pltpu.CompilerParams(vmem_limit_bytes=VMEM_LIMIT),
    )(*operands)


def on_device(total_stars, right_side, points, star_noise):
    rhs, own = right_side.shape
    amplitude = KERNEL_WEIGHT / total_stars
    vector, spare, copies = (rhs, own), (SPARE, own), (rhs * len(BLOCKS), own)

    packed, places = packed_inputs(right_side, points, star_noise[None, :])
    row_points = deal(places, PLANES)
    rights, kernels, pieces = [], [], None
    near, far = near_and_far(packed)
    for n, half in enumerate((near, far)):
        if n == 1:
            half, pieces = lax.optimization_barrier((half, pieces))
        for part in (half, exchange(half, "core", 1)):
            pieces, kernel = first_product(part, row_points, pieces, rhs, amplitude)
            kernels.append(kernel)
            rights.append(part)
    (first,) = small(update_one, rhs, [copies], deal(pieces, PLANES), packed)

    def product(vectors, lasts, scalars):
        mine = deal(vectors, LINES)
        other = exchange(mine, "core", 1)
        pieces = None
        for n, part in enumerate((mine, other)):
            pieces = next_product(
                part, rights[n::2], lasts[n], scalars, pieces, kernels[n::2], rhs, amplitude
            )
        return deal(pieces, PLANES), (mine, other)

    dealt, gathered = product(first, (None, None), None)
    third, second, scalars = small(
        update_two, rhs, [copies, vector, spare], dealt, packed, first
    )
    dealt, _ = product(third, gathered, scalars)
    dots, carry, kept = small(
        update_three,
        rhs,
        [spare, (5, rhs, own), spare],
        dealt,
        packed,
        first,
        second,
        third,
        scalars,
    )
    return tuple(small(update_four, rhs, [vector, vector], all_sum(dots), carry, kept))


def solution(mesh):
    placed = (P(None, AXES), P(None, AXES), P(AXES))

    def whole(right_side, points, star_noise):
        return jax.shard_map(
            functools.partial(on_device, right_side.shape[1]),
            mesh=mesh,
            in_specs=placed,
            out_specs=(P(None, AXES), P(None, AXES)),
            check_vma=False,
        )(right_side, points, star_noise)

    return whole
```

```python
import functools
import math

import jax
import jax.numpy as jnp
from jax import lax
from jax.experimental import pallas as pl
from jax.experimental.pallas import tpu as pltpu
from jax.sharding import PartitionSpec as P

QUAD_XX = 1.6
QUAD_XY = 0.5
QUAD_YY = 0.7
INVERSE_SQUARE = 25.0
KERNEL_WEIGHT = 2048.0

LOG2E = math.log2(math.e)
PX = math.sqrt(QUAD_XX * INVERSE_SQUARE)
PY = QUAD_XY * INVERSE_SQUARE / PX
QY = math.sqrt(QUAD_YY * INVERSE_SQUARE - PY * PY)
PX, PY, QY = PX * LOG2E, PY * LOG2E, QY * LOG2E

AXES = ("row", "col")
DEVICES = 256
LANES = 128
SPARE = 8
TILE = 256
VMEM_LIMIT = 24 * 1024 * 1024


def place(index):
    row, col = divmod(index, 16)
    y, z_lo = divmod(row, 4)
    x, rest = divmod(col, 4)
    z_hi, core = divmod(rest, 2)
    return {"x": x, "y": y, "z": z_hi * 4 + z_lo, "core": core}


def number(at):
    row = at["y"] * 4 + at["z"] % 4
    return row * 16 + at["x"] * 4 + (at["z"] // 4) * 2 + at["core"]


def bit_reversed(value, bits):
    return sum(((value >> b) & 1) << (bits - 1 - b) for b in range(bits))


def groups_along(*axes, key=None):
    groups = {}
    for index in range(DEVICES):
        rest = tuple(v for k, v in place(index).items() if k not in axes)
        groups.setdefault(rest, []).append(index)
    return [sorted(g, key=None if key is None else lambda i: key(place(i))) for g in groups.values()]


PLANES = groups_along("x", "y")
LINES = groups_along("z", key=lambda at: bit_reversed(at["z"], 3))
NEAR, FAR = (7, 2, 5), 1
BLOCKS = (0,) + NEAR + tuple(FAR ^ m for m in (0,) + NEAR)


def exchange(value, axis, mask):
    pairs = []
    for index in range(DEVICES):
        at = place(index)
        at[axis] ^= mask
        pairs.append((index, number(at)))
    return lax.ppermute(value, AXES, pairs)


def near_and_far(block):
    near = jnp.concatenate([block] + [exchange(block, "z", m) for m in NEAR], axis=0)
    return near, exchange(near, "z", FAR)


def deal(blocks, groups):
    count = len(groups[0])
    rows = blocks.shape[0] // count
    dealt = lax.all_to_all(
        blocks.reshape(count, rows, LANES), AXES, 0, 0, axis_index_groups=groups
    )
    return dealt.reshape(count * rows, LANES)


def all_sum(block):
    block = block + exchange(block, "core", 1)
    for groups in (LINES, PLANES):
        copies = jnp.broadcast_to(block[None], (len(groups[0]),) + block.shape)
        dealt = lax.all_to_all(copies, AXES, 0, 0, axis_index_groups=groups)
        block = jnp.sum(dealt, axis=0)
    return block


def split(vectors):
    high = vectors.astype(jnp.bfloat16)
    low = (vectors - high.astype(jnp.float32)).astype(jnp.bfloat16)
    return high, low


def as_columns(row, rhs):
    return jnp.broadcast_to(row, (LANES, LANES)).T[:rhs, :]


def put_pair(pair_ref, b, block, rhs):
    high, low = split(block)
    pair_ref[:rhs, b * LANES : (b + 1) * LANES] = high
    pair_ref[rhs:, b * LANES : (b + 1) * LANES] = low


def four_terms(pair, kernel, rhs):
    terms = jnp.dot(pair, kernel, preferred_element_type=jnp.float32)
    high, low = terms[:, :TILE], terms[:, TILE:]
    return high[:rhs] + ((high[rhs:] + low[:rhs]) + low[rhs:])


def first_body(rhs, amplitude, has_before, v_ref, rows_ref, *refs):
    before_ref, refs = (refs[0], refs[1:]) if has_before else (None, refs)
    out_ref, kernel_ref, pair_ref, p_ref, q_ref = refs
    step = rhs + SPARE
    tiles, stars, _ = kernel_ref.shape
    for b in range(stars // LANES):
        at = b * step + rhs
        put_pair(pair_ref, b, v_ref[at - rhs : at, :], rhs)
        x, y = v_ref[at : at + 1, :], v_ref[at + 1 : at + 2, :]
        rows = slice(b * LANES, (b + 1) * LANES)
        p_ref[rows, :] = as_columns(PX * x + PY * y, LANES)
        q_ref[rows, :] = as_columns(QY * y, LANES)

    for tile in range(tiles):
        product = jnp.zeros((rhs, TILE), jnp.float32)
        for j in range(0, stars, TILE):
            pieces = []
            for piece in range(TILE // LANES):
                at = (tile * (TILE // LANES) + piece) * SPARE
                x, y = rows_ref[at : at + 1, :], rows_ref[at + 1 : at + 2, :]
                delta_p = p_ref[j : j + TILE, :] - (PX * x + PY * y)
                delta_q = q_ref[j : j + TILE, :] - QY * y
                square = delta_p * delta_p + delta_q * delta_q
                distance = square * lax.rsqrt(jnp.maximum(square, 1e-30))
                pieces.append(split(jnp.exp2(-distance)))
            high = jnp.concatenate([h for h, _ in pieces], axis=1)
            low = jnp.concatenate([l for _, l in pieces], axis=1)
            both = jnp.concatenate([high, low], axis=1)
            kernel_ref[tile, j : j + TILE, :] = both
            product = product + four_terms(pair_ref[:, j : j + TILE], both, rhs)
        for piece in range(TILE // LANES):
            at = (tile * (TILE // LANES) + piece) * rhs
            part = product[:, piece * LANES : (piece + 1) * LANES] * amplitude
            if has_before:
                part = part + before_ref[at : at + rhs, :]
            out_ref[at : at + rhs, :] = part


def next_body(rhs, amplitude, has_last, has_before, v_ref, right_near_ref, right_far_ref, *refs):
    last_ref, scalars_ref, refs = (refs[0], refs[1], refs[2:]) if has_last else (None, None, refs)
    before_ref, refs = (refs[0], refs[1:]) if has_before else (None, refs)
    kernel_refs, out_ref, pair_ref = refs[:2], refs[2], refs[3]
    step = rhs + SPARE
    z_lo = lax.rem(lax.axis_index("row"), 4)
    z_hi = lax.rem(lax.div(lax.axis_index("col"), 2), 2)
    if has_last:
        alpha = as_columns(scalars_ref[0:1, :] / scalars_ref[1:2, :], rhs)
    norm = jnp.zeros((rhs, LANES), jnp.float32)
    curve = jnp.zeros((rhs, LANES), jnp.float32)
    half = len(BLOCKS) // 2
    for b, mask in enumerate(BLOCKS):
        lo, hi = lax.bitwise_xor(z_lo, mask % 4), lax.bitwise_xor(z_hi, mask // 4)
        place_in_line = lax.rem(lo, 2) * 4 + lax.div(lo, 2) * 2 + hi
        at = pl.multiple_of(place_in_line * rhs, rhs)
        block = v_ref[pl.ds(at, rhs), :]
        put_pair(pair_ref, b, block, rhs)
        right_ref = right_near_ref if b < half else right_far_ref
        residual = right_ref[b % half * step : b % half * step + rhs, :]
        if has_last:
            residual = residual - alpha * last_ref[pl.ds(at, rhs), :]
        norm = norm + residual * residual
        curve = curve + residual * block
    ones = jnp.ones((rhs, LANES), jnp.float32)
    dots = to_rows([dot(norm, ones), dot(curve, ones)], rhs)
    if has_before:
        dots = dots + before_ref[rhs:step, :]

    columns = half * LANES
    for tile in range(kernel_refs[0].shape[0]):
        near, far = (
            four_terms(pair_ref[:, n * columns : (n + 1) * columns], kernel_refs[n][tile], rhs)
            for n in range(2)
        )
        product = near + far
        for piece in range(TILE // LANES):
            at = (tile * (TILE // LANES) + piece) * step
            part = product[:, piece * LANES : (piece + 1) * LANES] * amplitude
            if has_before:
                part = part + before_ref[at : at + rhs, :]
            out_ref[at : at + rhs, :] = part
            out_ref[at + rhs : at + step, :] = dots


def kernel_call(body, outs, scratch, flops, operands):
    whole = pl.BlockSpec(memory_space=pltpu.VMEM)
    return pl.pallas_call(
        body,
        in_specs=[whole] * len(operands),
        out_specs=[whole] * len(outs),
        out_shape=outs,
        scratch_shapes=scratch,
        cost_estimate=pl.CostEstimate(flops=flops, bytes_accessed=0, transcendentals=0),
        compiler_params=pltpu.CompilerParams(vmem_limit_bytes=VMEM_LIMIT),
    )(*operands)


def first_product(part, row_points, before, rhs, amplitude):
    columns = part.shape[0] // (rhs + SPARE) * LANES
    pieces = row_points.shape[0] // SPARE
    outs = [
        jax.ShapeDtypeStruct((pieces * rhs, LANES), jnp.float32),
        jax.ShapeDtypeStruct((pieces * LANES // TILE, columns, 2 * TILE), jnp.bfloat16),
    ]
    scratch = [
        pltpu.VMEM((2 * rhs, columns), jnp.bfloat16),
        pltpu.VMEM((columns, LANES), jnp.float32),
        pltpu.VMEM((columns, LANES), jnp.float32),
    ]
    operands = [part, row_points] + ([] if before is None else [before])
    body = functools.partial(first_body, rhs, amplitude, before is not None)
    return kernel_call(body, outs, scratch, 3 << 30, operands)


def next_product(vectors, rights, last, scalars, before, kernels, rhs, amplitude):
    tiles, columns, _ = kernels[0].shape
    rows = tiles * (TILE // LANES) * (rhs + SPARE)
    outs = [jax.ShapeDtypeStruct((rows, LANES), jnp.float32)]
    scratch = [pltpu.VMEM((2 * rhs, 2 * columns), jnp.bfloat16)]
    operands = [vectors, *rights]
    operands += [] if last is None else [last, scalars]
    operands += [] if before is None else [before]
    operands += kernels
    body = functools.partial(next_body, rhs, amplitude, last is not None, before is not None)
    return kernel_call(body, outs, scratch, 1 << 31, operands)[0]


def dot(a, b):
    return jnp.sum(a * b, axis=1, keepdims=True)


def to_rows(columns, rhs):
    lane = lax.broadcasted_iota(jnp.int32, (rhs, LANES), 1)
    tile = jnp.zeros((rhs, LANES), jnp.float32)
    for i, column in enumerate(columns):
        tile = jnp.where(lane == i, column, tile)
    square = jnp.concatenate([tile, jnp.zeros((LANES - rhs, LANES), jnp.float32)], axis=0)
    return square.T[:SPARE, :]


def pack(rhs, right_ref, points_ref, noise_ref, out_ref, places_ref, spare_ref, semaphores):
    spare_ref[...] = jnp.zeros_like(spare_ref)
    copies = [
        pltpu.make_async_copy(right_ref, out_ref.at[pl.ds(0, rhs), :], semaphores.at[0]),
        pltpu.make_async_copy(points_ref, spare_ref.at[pl.ds(0, 2), :], semaphores.at[1]),
        pltpu.make_async_copy(noise_ref, spare_ref.at[pl.ds(2, 1), :], semaphores.at[2]),
    ]
    for copy in copies:
        copy.start()
    for copy in copies:
        copy.wait()
    spare = spare_ref[...]
    out_ref[rhs:, :] = spare
    for at in range(0, places_ref.shape[0], SPARE):
        places_ref[at : at + SPARE, :] = spare


def packed_inputs(right_side, points, noise):
    rhs, own = right_side.shape
    anywhere, whole = pl.BlockSpec(memory_space=pl.ANY), pl.BlockSpec(memory_space=pltpu.VMEM)
    return pl.pallas_call(
        functools.partial(pack, rhs),
        in_specs=[anywhere] * 3,
        out_specs=[whole] * 2,
        out_shape=[
            jax.ShapeDtypeStruct((rhs + SPARE, own), jnp.float32),
            jax.ShapeDtypeStruct((SPARE * len(PLANES[0]), own), jnp.float32),
        ],
        scratch_shapes=[pltpu.VMEM((SPARE, own), jnp.float32), pltpu.SemaphoreType.DMA((3,))],
        compiler_params=pltpu.CompilerParams(vmem_limit_bytes=60 * 1024 * 1024),
    )(right_side, points, noise)


def summed(dealt_ref, step):
    blocks = [dealt_ref[at : at + step, :] for at in range(0, dealt_ref.shape[0], step)]
    while len(blocks) > 1:
        blocks = [a + b for a, b in zip(blocks[::2], blocks[1::2])]
    return blocks[0]


def right_and_noise(packed_ref, rhs):
    return packed_ref[:rhs, :], packed_ref[rhs + 2 : rhs + 3, :]


def copy_out(copies_ref, vectors):
    rows = vectors.shape[0]
    for at in range(0, copies_ref.shape[0], rows):
        copies_ref[at : at + rows, :] = vectors


def update_one(rhs, dealt_ref, packed_ref, copies_ref):
    right, noise = right_and_noise(packed_ref, rhs)
    copy_out(copies_ref, summed(dealt_ref, rhs) + noise * right)


def update_two(rhs, dealt_ref, packed_ref, first_ref, copies_ref, second_ref, scalars_ref):
    right, noise = right_and_noise(packed_ref, rhs)
    w0 = first_ref[:rhs, :]
    image = summed(dealt_ref, rhs + SPARE)
    dots = image[rhs:, :]
    n0 = image[:rhs, :] + noise * w0
    alpha = as_columns(dots[0:1, :] / dots[1:2, :], rhs)
    copy_out(copies_ref, w0 - alpha * n0)
    second_ref[...] = n0
    scalars_ref[...] = dots


def update_three(rhs, dealt_ref, packed_ref, first_ref, second_ref, third_ref, scalars_ref, dots_ref, carry_ref, kept_ref):
    right, noise = right_and_noise(packed_ref, rhs)
    w0 = first_ref[:rhs, :]
    n0 = second_ref[...]
    w1 = third_ref[:rhs, :]
    image = summed(dealt_ref, rhs + SPARE)
    dots = image[rhs:, :]
    n1 = image[:rhs, :] + noise * w1
    norm0, curve0 = scalars_ref[0:1, :], scalars_ref[1:2, :]
    norm1, curve1 = dots[0:1, :], dots[1:2, :]
    alpha0_row = norm0 / curve0
    beta1_row = norm1 / norm0
    alpha1_row = norm1 / (curve1 - beta1_row * norm1 / alpha0_row)
    alpha0, beta1, alpha1 = (as_columns(row, rhs) for row in (alpha0_row, beta1_row, alpha1_row))
    r1 = right - alpha0 * w0
    s1 = w1 + beta1 * w0
    p1 = r1 + beta1 * right
    z1 = n1 + beta1 * n0
    r2 = r1 - alpha1 * s1
    w2 = w1 - alpha1 * z1
    dots_ref[...] = to_rows([dot(r2, r2), dot(r2, w2)], rhs)
    carry_ref[0] = alpha0 * right + alpha1 * p1
    carry_ref[1] = r2
    carry_ref[2] = p1
    carry_ref[3] = s1
    carry_ref[4] = w2
    kept_ref[...] = jnp.concatenate(
        [norm1, alpha1_row, jnp.zeros((SPARE - 2, LANES), jnp.float32)], axis=0
    )


def update_four(rhs, dots_ref, carry_ref, kept_ref, solution_ref, residual_ref):
    norm2, curve2 = dots_ref[0:1, :], dots_ref[1:2, :]
    norm1, alpha1 = kept_ref[0:1, :], kept_ref[1:2, :]
    beta2_row = norm2 / norm1
    alpha2 = as_columns(norm2 / (curve2 - beta2_row * norm2 / alpha1), rhs)
    beta2 = as_columns(beta2_row, rhs)
    r2 = carry_ref[1]
    solution_ref[...] = carry_ref[0] + alpha2 * (r2 + beta2 * carry_ref[2])
    residual_ref[...] = r2 - alpha2 * (carry_ref[4] + beta2 * carry_ref[3])


def small(body, rhs, shapes, *operands):
    outs = [jax.ShapeDtypeStruct(s, jnp.float32) for s in shapes]
    return pl.pallas_call(
        functools.partial(body, rhs),
        out_shape=outs,
        compiler_params=pltpu.CompilerParams(vmem_limit_bytes=VMEM_LIMIT),
    )(*operands)


def on_device(total_stars, right_side, points, star_noise):
    rhs, own = right_side.shape
    amplitude = KERNEL_WEIGHT / total_stars
    vector, spare, copies = (rhs, own), (SPARE, own), (rhs * len(BLOCKS), own)

    packed, places = packed_inputs(right_side, points, star_noise[None, :])
    row_points = deal(places, PLANES)
    rights, kernels, pieces = [], [], None
    near, far = near_and_far(packed)
    for n, half in enumerate((near, far)):
        if n == 1:
            half, pieces = lax.optimization_barrier((half, pieces))
        for part in (half, exchange(half, "core", 1)):
            pieces, kernel = first_product(part, row_points, pieces, rhs, amplitude)
            kernels.append(kernel)
            rights.append(part)
    (first,) = small(update_one, rhs, [copies], deal(pieces, PLANES), packed)

    def product(vectors, lasts, scalars):
        mine = deal(vectors, LINES)
        other = exchange(mine, "core", 1)
        pieces = None
        for n, part in enumerate((mine, other)):
            pieces = next_product(
                part, rights[n::2], lasts[n], scalars, pieces, kernels[n::2], rhs, amplitude
            )
        return deal(pieces, PLANES), (mine, other)

    dealt, gathered = product(first, (None, None), None)
    third, second, scalars = small(
        update_two, rhs, [copies, vector, spare], dealt, packed, first
    )
    dealt, _ = product(third, gathered, scalars)
    dots, carry, kept = small(
        update_three,
        rhs,
        [spare, (5, rhs, own), spare],
        dealt,
        packed,
        first,
        second,
        third,
        scalars,
    )
    return tuple(small(update_four, rhs, [vector, vector], all_sum(dots), carry, kept))


def solution(mesh):
    placed = (P(None, AXES), P(None, AXES), P(AXES))

    def whole(right_side, points, star_noise):
        return jax.shard_map(
            functools.partial(on_device, right_side.shape[1]),
            mesh=mesh,
            in_specs=placed,
            out_specs=(P(None, AXES), P(None, AXES)),
            check_vma=False,
        )(right_side, points, star_noise)

    return whole
```

```python
import functools
import math

import jax
import jax.numpy as jnp
from jax import lax
from jax.experimental import pallas as pl
from jax.experimental.pallas import tpu as pltpu
from jax.sharding import PartitionSpec as P

QUAD_XX = 1.6
QUAD_XY = 0.5
QUAD_YY = 0.7
INVERSE_SQUARE = 25.0
KERNEL_WEIGHT = 2048.0

LOG2E = math.log2(math.e)
PX = math.sqrt(QUAD_XX * INVERSE_SQUARE)
PY = QUAD_XY * INVERSE_SQUARE / PX
QY = math.sqrt(QUAD_YY * INVERSE_SQUARE - PY * PY)
PX, PY, QY = PX * LOG2E, PY * LOG2E, QY * LOG2E

AXES = ("row", "col")
DEVICES = 256
LANES = 128
SPARE = 8
TILE = 256
VMEM_LIMIT = 24 * 1024 * 1024


def place(index):
    row, col = divmod(index, 16)
    y, z_lo = divmod(row, 4)
    x, rest = divmod(col, 4)
    z_hi, core = divmod(rest, 2)
    return {"x": x, "y": y, "z": z_hi * 4 + z_lo, "core": core}


def number(at):
    row = at["y"] * 4 + at["z"] % 4
    return row * 16 + at["x"] * 4 + (at["z"] // 4) * 2 + at["core"]


def bit_reversed(value, bits):
    return sum(((value >> b) & 1) << (bits - 1 - b) for b in range(bits))


def groups_along(*axes, key=None):
    groups = {}
    for index in range(DEVICES):
        rest = tuple(v for k, v in place(index).items() if k not in axes)
        groups.setdefault(rest, []).append(index)
    return [sorted(g, key=None if key is None else lambda i: key(place(i))) for g in groups.values()]


PLANES = groups_along("x", "y")
LINES = groups_along("z", key=lambda at: bit_reversed(at["z"], 3))
NEAR, FAR = (7, 2, 5), 1
BLOCKS = (0,) + NEAR + tuple(FAR ^ m for m in (0,) + NEAR)


def exchange(value, axis, mask):
    pairs = []
    for index in range(DEVICES):
        at = place(index)
        at[axis] ^= mask
        pairs.append((index, number(at)))
    return lax.ppermute(value, AXES, pairs)


def near_and_far(block):
    near = jnp.concatenate([block] + [exchange(block, "z", m) for m in NEAR], axis=0)
    return near, exchange(near, "z", FAR)


def deal(blocks, groups):
    count = len(groups[0])
    rows = blocks.shape[0] // count
    dealt = lax.all_to_all(
        blocks.reshape(count, rows, LANES), AXES, 0, 0, axis_index_groups=groups
    )
    return dealt.reshape(count * rows, LANES)


def all_sum(block):
    block = block + exchange(block, "core", 1)
    for groups in (PLANES, LINES):
        copies = jnp.broadcast_to(block[None], (len(groups[0]),) + block.shape)
        dealt = lax.all_to_all(copies, AXES, 0, 0, axis_index_groups=groups)
        block = jnp.sum(dealt, axis=0)
    return block


def split(vectors):
    high = vectors.astype(jnp.bfloat16)
    low = (vectors - high.astype(jnp.float32)).astype(jnp.bfloat16)
    return high, low


def as_columns(row, rhs):
    return jnp.broadcast_to(row, (LANES, LANES)).T[:rhs, :]


def put_pair(pair_ref, b, block, rhs):
    high, low = split(block)
    pair_ref[:rhs, b * LANES : (b + 1) * LANES] = high
    pair_ref[rhs:, b * LANES : (b + 1) * LANES] = low


def four_terms(pair, kernel, rhs):
    terms = jnp.dot(pair, kernel, preferred_element_type=jnp.float32)
    high, low = terms[:, :TILE], terms[:, TILE:]
    return high[:rhs] + ((high[rhs:] + low[:rhs]) + low[rhs:])


def first_body(rhs, amplitude, has_before, v_ref, rows_ref, *refs):
    before_ref, refs = (refs[0], refs[1:]) if has_before else (None, refs)
    out_ref, kernel_ref, pair_ref, p_ref, q_ref = refs
    step = rhs + SPARE
    tiles, stars, _ = kernel_ref.shape
    for b in range(stars // LANES):
        at = b * step + rhs
        put_pair(pair_ref, b, v_ref[at - rhs : at, :], rhs)
        x, y = v_ref[at : at + 1, :], v_ref[at + 1 : at + 2, :]
        rows = slice(b * LANES, (b + 1) * LANES)
        p_ref[rows, :] = as_columns(PX * x + PY * y, LANES)
        q_ref[rows, :] = as_columns(QY * y, LANES)

    for tile in range(tiles):
        product = jnp.zeros((rhs, TILE), jnp.float32)
        for j in range(0, stars, TILE):
            pieces = []
            for piece in range(TILE // LANES):
                at = (tile * (TILE // LANES) + piece) * SPARE
                x, y = rows_ref[at : at + 1, :], rows_ref[at + 1 : at + 2, :]
                delta_p = p_ref[j : j + TILE, :] - (PX * x + PY * y)
                delta_q = q_ref[j : j + TILE, :] - QY * y
                square = delta_p * delta_p + delta_q * delta_q
                distance = square * lax.rsqrt(jnp.maximum(square, 1e-30))
                pieces.append(split(jnp.exp2(-distance)))
            high = jnp.concatenate([h for h, _ in pieces], axis=1)
            low = jnp.concatenate([l for _, l in pieces], axis=1)
            both = jnp.concatenate([high, low], axis=1)
            kernel_ref[tile, j : j + TILE, :] = both
            product = product + four_terms(pair_ref[:, j : j + TILE], both, rhs)
        for piece in range(TILE // LANES):
            at = (tile * (TILE // LANES) + piece) * rhs
            part = product[:, piece * LANES : (piece + 1) * LANES] * amplitude
            if has_before:
                part = part + before_ref[at : at + rhs, :]
            out_ref[at : at + rhs, :] = part


def next_body(rhs, amplitude, has_last, has_before, v_ref, right_near_ref, right_far_ref, *refs):
    last_ref, scalars_ref, refs = (refs[0], refs[1], refs[2:]) if has_last else (None, None, refs)
    before_ref, refs = (refs[0], refs[1:]) if has_before else (None, refs)
    kernel_refs, out_ref, pair_ref = refs[:2], refs[2], refs[3]
    step = rhs + SPARE
    z_lo = lax.rem(lax.axis_index("row"), 4)
    z_hi = lax.rem(lax.div(lax.axis_index("col"), 2), 2)
    if has_last:
        alpha = as_columns(scalars_ref[0:1, :] / scalars_ref[1:2, :], rhs)
    norm = jnp.zeros((rhs, LANES), jnp.float32)
    curve = jnp.zeros((rhs, LANES), jnp.float32)
    half = len(BLOCKS) // 2
    for b, mask in enumerate(BLOCKS):
        lo, hi = lax.bitwise_xor(z_lo, mask % 4), lax.bitwise_xor(z_hi, mask // 4)
        place_in_line = lax.rem(lo, 2) * 4 + lax.div(lo, 2) * 2 + hi
        at = pl.multiple_of(place_in_line * rhs, rhs)
        block = v_ref[pl.ds(at, rhs), :]
        put_pair(pair_ref, b, block, rhs)
        right_ref = right_near_ref if b < half else right_far_ref
        residual = right_ref[b % half * step : b % half * step + rhs, :]
        if has_last:
            residual = residual - alpha * last_ref[pl.ds(at, rhs), :]
        norm = norm + residual * residual
        curve = curve + residual * block
    ones = jnp.ones((rhs, LANES), jnp.float32)
    dots = to_rows([dot(norm, ones), dot(curve, ones)], rhs)
    if has_before:
        dots = dots + before_ref[rhs:step, :]

    columns = half * LANES
    for tile in range(kernel_refs[0].shape[0]):
        near, far = (
            four_terms(pair_ref[:, n * columns : (n + 1) * columns], kernel_refs[n][tile], rhs)
            for n in range(2)
        )
        product = near + far
        for piece in range(TILE // LANES):
            at = (tile * (TILE // LANES) + piece) * step
            part = product[:, piece * LANES : (piece + 1) * LANES] * amplitude
            if has_before:
                part = part + before_ref[at : at + rhs, :]
            out_ref[at : at + rhs, :] = part
            out_ref[at + rhs : at + step, :] = dots


def kernel_call(body, outs, scratch, flops, operands):
    whole = pl.BlockSpec(memory_space=pltpu.VMEM)
    return pl.pallas_call(
        body,
        in_specs=[whole] * len(operands),
        out_specs=[whole] * len(outs),
        out_shape=outs,
        scratch_shapes=scratch,
        cost_estimate=pl.CostEstimate(flops=flops, bytes_accessed=0, transcendentals=0),
        compiler_params=pltpu.CompilerParams(vmem_limit_bytes=VMEM_LIMIT),
    )(*operands)


def first_product(part, row_points, before, rhs, amplitude):
    columns = part.shape[0] // (rhs + SPARE) * LANES
    pieces = row_points.shape[0] // SPARE
    outs = [
        jax.ShapeDtypeStruct((pieces * rhs, LANES), jnp.float32),
        jax.ShapeDtypeStruct((pieces * LANES // TILE, columns, 2 * TILE), jnp.bfloat16),
    ]
    scratch = [
        pltpu.VMEM((2 * rhs, columns), jnp.bfloat16),
        pltpu.VMEM((columns, LANES), jnp.float32),
        pltpu.VMEM((columns, LANES), jnp.float32),
    ]
    operands = [part, row_points] + ([] if before is None else [before])
    body = functools.partial(first_body, rhs, amplitude, before is not None)
    return kernel_call(body, outs, scratch, 3 << 30, operands)


def next_product(vectors, rights, last, scalars, before, kernels, rhs, amplitude):
    tiles, columns, _ = kernels[0].shape
    rows = tiles * (TILE // LANES) * (rhs + SPARE)
    outs = [jax.ShapeDtypeStruct((rows, LANES), jnp.float32)]
    scratch = [pltpu.VMEM((2 * rhs, 2 * columns), jnp.bfloat16)]
    operands = [vectors, *rights]
    operands += [] if last is None else [last, scalars]
    operands += [] if before is None else [before]
    operands += kernels
    body = functools.partial(next_body, rhs, amplitude, last is not None, before is not None)
    return kernel_call(body, outs, scratch, 1 << 31, operands)[0]


def dot(a, b):
    return jnp.sum(a * b, axis=1, keepdims=True)


def to_rows(columns, rhs):
    lane = lax.broadcasted_iota(jnp.int32, (rhs, LANES), 1)
    tile = jnp.zeros((rhs, LANES), jnp.float32)
    for i, column in enumerate(columns):
        tile = jnp.where(lane == i, column, tile)
    square = jnp.concatenate([tile, jnp.zeros((LANES - rhs, LANES), jnp.float32)], axis=0)
    return square.T[:SPARE, :]


def summed(dealt_ref, step):
    blocks = [dealt_ref[at : at + step, :] for at in range(0, dealt_ref.shape[0], step)]
    while len(blocks) > 1:
        blocks = [a + b for a, b in zip(blocks[::2], blocks[1::2])]
    return blocks[0]


def right_and_noise(packed_ref, rhs):
    return packed_ref[:rhs, :], packed_ref[rhs + 2 : rhs + 3, :]


def copy_out(copies_ref, vectors):
    rows = vectors.shape[0]
    for at in range(0, copies_ref.shape[0], rows):
        copies_ref[at : at + rows, :] = vectors


def update_one(rhs, dealt_ref, packed_ref, copies_ref):
    right, noise = right_and_noise(packed_ref, rhs)
    copy_out(copies_ref, summed(dealt_ref, rhs) + noise * right)


def update_two(rhs, dealt_ref, packed_ref, first_ref, copies_ref, second_ref, scalars_ref):
    right, noise = right_and_noise(packed_ref, rhs)
    w0 = first_ref[:rhs, :]
    image = summed(dealt_ref, rhs + SPARE)
    dots = image[rhs:, :]
    n0 = image[:rhs, :] + noise * w0
    alpha = as_columns(dots[0:1, :] / dots[1:2, :], rhs)
    copy_out(copies_ref, w0 - alpha * n0)
    second_ref[...] = n0
    scalars_ref[...] = dots


def update_three(rhs, dealt_ref, packed_ref, first_ref, second_ref, third_ref, scalars_ref, dots_ref, carry_ref, kept_ref):
    right, noise = right_and_noise(packed_ref, rhs)
    w0 = first_ref[:rhs, :]
    n0 = second_ref[...]
    w1 = third_ref[:rhs, :]
    image = summed(dealt_ref, rhs + SPARE)
    dots = image[rhs:, :]
    n1 = image[:rhs, :] + noise * w1
    norm0, curve0 = scalars_ref[0:1, :], scalars_ref[1:2, :]
    norm1, curve1 = dots[0:1, :], dots[1:2, :]
    alpha0_row = norm0 / curve0
    beta1_row = norm1 / norm0
    alpha1_row = norm1 / (curve1 - beta1_row * norm1 / alpha0_row)
    alpha0, beta1, alpha1 = (as_columns(row, rhs) for row in (alpha0_row, beta1_row, alpha1_row))
    r1 = right - alpha0 * w0
    s1 = w1 + beta1 * w0
    p1 = r1 + beta1 * right
    z1 = n1 + beta1 * n0
    r2 = r1 - alpha1 * s1
    w2 = w1 - alpha1 * z1
    dots_ref[...] = to_rows([dot(r2, r2), dot(r2, w2)], rhs)
    carry_ref[0] = alpha0 * right + alpha1 * p1
    carry_ref[1] = r2
    carry_ref[2] = p1
    carry_ref[3] = s1
    carry_ref[4] = w2
    kept_ref[...] = jnp.concatenate(
        [norm1, alpha1_row, jnp.zeros((SPARE - 2, LANES), jnp.float32)], axis=0
    )


def update_four(rhs, dots_ref, carry_ref, kept_ref, solution_ref, residual_ref):
    norm2, curve2 = dots_ref[0:1, :], dots_ref[1:2, :]
    norm1, alpha1 = kept_ref[0:1, :], kept_ref[1:2, :]
    beta2_row = norm2 / norm1
    alpha2 = as_columns(norm2 / (curve2 - beta2_row * norm2 / alpha1), rhs)
    beta2 = as_columns(beta2_row, rhs)
    r2 = carry_ref[1]
    solution_ref[...] = carry_ref[0] + alpha2 * (r2 + beta2 * carry_ref[2])
    residual_ref[...] = r2 - alpha2 * (carry_ref[4] + beta2 * carry_ref[3])


def small(body, rhs, shapes, *operands):
    outs = [jax.ShapeDtypeStruct(s, jnp.float32) for s in shapes]
    return pl.pallas_call(
        functools.partial(body, rhs),
        out_shape=outs,
        compiler_params=pltpu.CompilerParams(vmem_limit_bytes=VMEM_LIMIT),
    )(*operands)


def on_device(total_stars, right_side, points, star_noise):
    rhs, own = right_side.shape
    amplitude = KERNEL_WEIGHT / total_stars
    vector, spare, copies = (rhs, own), (SPARE, own), (rhs * len(BLOCKS), own)

    empty = jnp.zeros((SPARE - 3, own), jnp.float32)
    packed = jnp.concatenate([right_side, points, star_noise[None, :], empty], axis=0)
    packed = lax.optimization_barrier(packed)
    row_points = deal(jnp.tile(packed[rhs:], (len(PLANES[0]), 1)), PLANES)
    rights, kernels, pieces = [], [], None
    near, far = near_and_far(packed)
    for n, half in enumerate((near, far)):
        if n == 1:
            half, pieces = lax.optimization_barrier((half, pieces))
        for part in (half, exchange(half, "core", 1)):
            pieces, kernel = first_product(part, row_points, pieces, rhs, amplitude)
            kernels.append(kernel)
            rights.append(part)
    (first,) = small(update_one, rhs, [copies], deal(pieces, PLANES), packed)

    def product(vectors, lasts, scalars):
        mine = deal(vectors, LINES)
        other = exchange(mine, "core", 1)
        pieces = None
        for n, part in enumerate((mine, other)):
            pieces = next_product(
                part, rights[n::2], lasts[n], scalars, pieces, kernels[n::2], rhs, amplitude
            )
        return deal(pieces, PLANES), (mine, other)

    dealt, gathered = product(first, (None, None), None)
    third, second, scalars = small(
        update_two, rhs, [copies, vector, spare], dealt, packed, first
    )
    dealt, _ = product(third, gathered, scalars)
    dots, carry, kept = small(
        update_three,
        rhs,
        [spare, (5, rhs, own), spare],
        dealt,
        packed,
        first,
        second,
        third,
        scalars,
    )
    return tuple(small(update_four, rhs, [vector, vector], all_sum(dots), carry, kept))


def solution(mesh):
    placed = (P(None, AXES), P(None, AXES), P(AXES))

    def whole(right_side, points, star_noise):
        return jax.shard_map(
            functools.partial(on_device, right_side.shape[1]),
            mesh=mesh,
            in_specs=placed,
            out_specs=(P(None, AXES), P(None, AXES)),
            check_vma=False,
        )(right_side, points, star_noise)

    return whole
```
